32 devices in a mesh: rep: 2 (over x), fsdp: 2 (over y), ctx: 8 (over z, core).
Axes of the slice: x: 2, y: 2, z: 4, core: 2. Of those that a mesh axis runs over, the one named last changes fastest.
Arguments:
- tokens: bfloat16 [8, 2048, 1024], P(('rep', 'fsdp'), 'ctx'), may hold values from -6 to 6
- segments: int32 [8, 2048], P(('rep', 'fsdp')), may hold values from 0 to 16, as said below
- expand_weight: bfloat16 [2, 1024, 4384], P(None, 'fsdp'), may hold values from -0.1875 to 0.1875
- reduce_weight: bfloat16 [2, 2048, 1024], P(None, 'fsdp'), may hold values from -0.125 to 0.125
- filter_taps: bfloat16 [2, 4, 2304], P(None, None, 'fsdp'), may hold values from -3 to 3
- filter_offset: bfloat16 [2, 2304], P(None, 'fsdp'), may hold values from -1.5 to 1.5
- step_bias: bfloat16 [2, 32], P(None, 'fsdp'), may hold values from -4 to -2
- decay_rate: bfloat16 [2, 32], P(None, 'fsdp'), may hold values from 0 to 0.25, as said below
- skip_gain: bfloat16 [2, 32], P(None, 'fsdp'), may hold values from 0.5 to 1.5
- norm_gain: bfloat16 [2, 1024], P(None, 'fsdp'), may hold values from 0.5 to 1.5
- gate_gain: bfloat16 [2, 2048], P(None, 'fsdp'), may hold values from 0.5 to 1.5
- cotangent: bfloat16 [8, 2048, 1024], P(('rep', 'fsdp'), 'ctx'), may hold values from -6 to 6
Outputs:
- layer_out: bfloat16 [8, 2048, 1024], P(('rep', 'fsdp'), 'ctx')
- token_grads: bfloat16 [8, 2048, 1024], P(('rep', 'fsdp'), 'ctx')
- expand_grads: float32 [2, 1024, 4384], P(None, 'fsdp')
- reduce_grads: float32 [2, 2048, 1024], P(None, 'fsdp')
- filter_grads: float32 [2, 4, 2304], P(None, None, 'fsdp')
- offset_grads: float32 [2, 2304], P(None, 'fsdp')
- step_grads: float32 [2, 32], P(None, 'fsdp')
- decay_grads: float32 [2, 32], P(None, 'fsdp')
- skip_grads: float32 [2, 32], P(None, 'fsdp')
- norm_grads: float32 [2, 1024], P(None, 'fsdp')
- gating_grads: float32 [2, 2048], P(None, 'fsdp')
The draws below stay inside these ranges and needn't reach their ends.
Inputs may be any that keep to these rules, and one draw needn't show every extreme that they name: `segments`: along each sequence the ids start at 0 and rise by 0 or 1 from one token to the next; tokens with equal ids form one document. Of each 2 consecutive sequences, one holds exactly 2 documents, the first of which ends within the last 256 tokens, and every other one holds exactly 17 documents. `decay_rate`: Positive.
All inputs are finite; a program needn't handle non-finite values.
Results may differ from the reference program's by a relative error of at most 0.019.
The reference program's roundings to bfloat16 on the way count: a program that leaves them out, or rounds other values in their place, can miss the bound.
Values may be sent and summed in bfloat16 or wider, within the bound.
No kernel may reach another device: no remote copies, remote signals or barrier semaphores. Data moves between devices by JAX's collectives and lax.ppermute only.
A program may use at most 448 MiB of HBM per device.

```python
import math
import jax
import jax.numpy as jnp
from jax import lax

D = 1024
H = 32
P_SIZE = 64
N = 128
CONV = 4
SPAN = 256
LAYERS = 2
SEQS = 2
DI = 2048
CH = 2304
E = 4384
LENGTH = 2048
BATCH = 8


def draw_segments(key, part):
    key = jax.random.fold_in(key, 11)
    score_key, pick_key, place_key = jax.random.split(key, 3)
    boundaries = 2 * (LENGTH // SPAN)
    raw_scores = jax.random.randint(score_key, (BATCH, LENGTH - 1), 0, LENGTH)
    scores = raw_scores * LENGTH + jnp.arange(LENGTH - 1, dtype=jnp.int32)[None, :]
    order = jnp.argsort(scores, axis=1, stable=True)
    ranks = jnp.argsort(order, axis=1, stable=True)
    flags = (ranks < boundaries).astype(jnp.int32)
    starts = jnp.concatenate([jnp.zeros((BATCH, 1), jnp.int32), flags], axis=1)
    chosen = jax.random.randint(pick_key, (BATCH // SEQS,), 0, SEQS)
    places = jax.random.randint(place_key, (BATCH // SEQS,), LENGTH - SPAN + 1, LENGTH)
    row_index = jnp.arange(BATCH)
    single = row_index % SEQS == chosen[row_index // SEQS]
    positions = jnp.arange(LENGTH, dtype=jnp.int32)[None, :]
    lone = (positions == places[row_index // SEQS][:, None]).astype(jnp.int32)
    starts = jnp.where(single[:, None], lone, starts)
    return jnp.cumsum(starts, axis=1).astype(jnp.int32)


def draw_decay_rate(key, part):
    key = jax.random.fold_in(key, 7)
    lower = math.log(2.0 / LENGTH)
    upper = math.log(0.25)
    return jnp.exp(jax.random.uniform(key, (LAYERS, H), jnp.float32, lower, upper)).astype(jnp.bfloat16)


def shard_levels(stream_key, extent, cuts, low, high):
    factor_of = 1.0
    for dim, shards_of in cuts:
        steps = jax.random.uniform(jax.random.fold_in(jax.random.fold_in(stream_key, 6), dim), (shards_of,), jnp.float32, low / len(cuts), high / len(cuts))
        factor_of = factor_of * jnp.repeat(jnp.exp(steps), extent[dim] // shards_of).reshape((-1,) + (1,) * (len(extent) - 1 - dim))
    return factor_of


def noise(rng, extent, spread, limit, cuts=(), held_as=jnp.bfloat16):
    values = spread * jax.random.normal(rng, extent, jnp.float32)
    if cuts:
        values = values * shard_levels(rng, extent, cuts, -0.22, 0.18)
    return jnp.clip(values, -limit, limit).astype(held_as)


def setup_inputs(seed: int = 0) -> dict:
    arg_keys = jax.random.split(jax.random.key(seed), 13)
    tokens = noise(arg_keys[0], (BATCH, LENGTH, D), 1.0, 6.0, ((0, 4), (1, 8)))
    segments = draw_segments(jax.random.fold_in(arg_keys[12], 71), 0)
    expand_weight = noise(arg_keys[2], (LAYERS, D, E), D ** -0.5, 0.1875, ((1, 2),))
    reduce_weight = noise(arg_keys[3], (LAYERS, DI, D), DI ** -0.5, 0.125, ((1, 2),))
    filter_taps = noise(arg_keys[4], (LAYERS, CONV, CH), CONV ** -0.5, 3.0, ((2, 2),))
    filter_offset = noise(arg_keys[5], (LAYERS, CH), 0.3, 1.5, ((1, 2),))
    step_bias = jnp.clip(-4.0 + 2.0 * jax.random.uniform(arg_keys[6], (LAYERS, H), jnp.float32) ** shard_levels(arg_keys[6], (LAYERS, H), ((1, 2),), -0.2, 0.2), -4.0, -2.0).astype(jnp.bfloat16)
    decay_rate = draw_decay_rate(jax.random.fold_in(arg_keys[12], 71), 0)
    skip_gain = jnp.clip(0.5 + 1.0 * jax.random.uniform(arg_keys[8], (LAYERS, H), jnp.float32) ** shard_levels(arg_keys[8], (LAYERS, H), ((1, 2),), -0.2, 0.2), 0.5, 1.5).astype(jnp.bfloat16)
    norm_gain = jnp.clip(1.0 + 0.1 * jax.random.normal(arg_keys[9], (LAYERS, D), jnp.float32), 0.5, 1.5).astype(jnp.bfloat16)
    gate_gain = jnp.clip(1.0 + 0.1 * jax.random.normal(arg_keys[10], (LAYERS, DI), jnp.float32), 0.5, 1.5).astype(jnp.bfloat16)
    cotangent = noise(arg_keys[11], (BATCH, LENGTH, D), 1.0, 6.0, ((0, 4), (1, 8)))
    return dict(tokens=tokens, segments=segments, expand_weight=expand_weight, reduce_weight=reduce_weight, filter_taps=filter_taps, filter_offset=filter_offset, step_bias=step_bias, decay_rate=decay_rate, skip_gain=skip_gain, norm_gain=norm_gain, gate_gain=gate_gain, cotangent=cotangent)


EPSILON = 1e-05
FULL_PRECISION = lax.Precision.HIGHEST

@jax.custom_vjp
def low(v):
    return lax.optimization_barrier(v.astype(jnp.bfloat16)).astype(jnp.float32)

@jax.custom_vjp
def low_back(v):
    return v

def low_keep(v):
    return (low(v), None)

def low_pass(kept, grad):
    return (grad,)

def back_keep(v):
    return (v, None)

def back_low(kept, grad):
    return (low(grad),)
low.defvjp(low_keep, low_pass)
low_back.defvjp(back_keep, back_low)

def rms_scale(values, gain):
    return values * lax.rsqrt(lax.optimization_barrier(jnp.mean(values * values, axis=-1, keepdims=True)) + EPSILON) * gain

def block_recurrence(carry_state, values, b_keys, c_reads, step_size, segment, before, decay_rate, skip_gain):
    block_rows = segment.shape[0]
    log_decay = jnp.cumsum(-(step_size * decay_rate[None, :]), axis=0).T
    joined = (segment[0] == before).astype(jnp.float32)
    row_index = lax.broadcasted_iota(jnp.int32, (block_rows, block_rows), 0)
    col_index = lax.broadcasted_iota(jnp.int32, (block_rows, block_rows), 1)
    causal = (segment[:, None] == segment[None, :]) & (row_index >= col_index)
    gap_logs = log_decay[:, :, None] - log_decay[:, None, :]
    decay_mask = jnp.where(causal[None], jnp.exp(jnp.where(causal[None], gap_logs, 0.0)), 0.0)
    scores = jnp.dot(c_reads, b_keys.T, precision=FULL_PRECISION)
    weights = decay_mask * scores[None] * step_size.T[:, None, :]
    within = jnp.einsum('hts,shp->thp', weights, values, precision=FULL_PRECISION)
    from_start = jnp.exp(log_decay) * joined * (segment == segment[0]).astype(jnp.float32)[None, :]
    carried = jnp.einsum('tn,hpn,ht->thp', c_reads, carry_state, from_start, precision=FULL_PRECISION)
    outputs = within + carried + values * skip_gain[None, :, None]
    to_end = jnp.exp(log_decay[:, -1:] - log_decay) * (segment == segment[-1]).astype(jnp.float32)[None, :] * step_size.T
    added_state = jnp.einsum('hs,shp,sn->hpn', to_end, values, b_keys, precision=FULL_PRECISION)
    block_decay = jnp.exp(log_decay[:, -1]) * joined * (segment[-1] == segment[0]).astype(jnp.float32)
    return (block_decay[:, None, None] * carry_state + added_state, outputs.reshape(block_rows, DI))

def mixer_layer(resid, segment, expand_w, reduce_w, taps, offsets, step_bias, decay_rate, skip_gain, norm_gain, gate_gain):
    groups = resid.shape[0]
    length = resid.shape[1]
    normed = low(rms_scale(resid, norm_gain))
    mixed = low_back(low(jnp.einsum('gtd,de->gte', normed, expand_w, precision=FULL_PRECISION)))
    gate_part = mixed[..., :DI]
    conv_part = mixed[..., DI:DI + CH]
    step_part = mixed[..., DI + CH:]
    padded = jnp.pad(conv_part, ((0, 0), (CONV - 1, 0), (0, 0)))
    seg_padded = jnp.concatenate([jnp.full((groups, CONV - 1), -1, jnp.int32), segment], axis=1)
    filtered = jnp.broadcast_to(offsets, conv_part.shape)
    for tap_index in range(CONV):
        same = (seg_padded[:, tap_index:tap_index + length] == segment).astype(jnp.float32)
        filtered = filtered + taps[tap_index] * padded[:, tap_index:tap_index + length] * same[..., None]
    active = jax.nn.silu(filtered)
    blocks = length // SPAN
    values = active[..., :DI].reshape(groups, blocks, SPAN, H, P_SIZE)
    b_keys = active[..., DI:DI + N].reshape(groups, blocks, SPAN, N)
    c_reads = active[..., DI + N:].reshape(groups, blocks, SPAN, N)
    step_size = jax.nn.softplus(step_part + step_bias).reshape(groups, blocks, SPAN, H)
    seg_blocks = segment.reshape(groups, blocks, SPAN)
    before = seg_padded[:, CONV - 2:CONV - 2 + length].reshape(groups, blocks, SPAN)[:, :, 0]
    pieces = tuple((jnp.moveaxis(item, 1, 0) for item in (values, b_keys, c_reads, step_size, seg_blocks, before)))

    def scan_step(carry_state, block_pieces):
        return jax.vmap(block_recurrence, in_axes=(0, 0, 0, 0, 0, 0, 0, None, None))(carry_state, *block_pieces, decay_rate, skip_gain)
    start_state = jnp.zeros((groups, H, P_SIZE, N), jnp.float32)
    _, outputs = lax.scan(jax.checkpoint(scan_step), start_state, pieces)
    outputs = jnp.moveaxis(outputs, 0, 1).reshape(groups, length, DI)
    gated = outputs * jax.nn.silu(gate_part)
    out_in = low(rms_scale(gated, gate_gain))
    branch = low_back(jnp.einsum('gti,id->gtd', out_in, reduce_w, precision=FULL_PRECISION))
    return resid + branch

def reference(tokens, segments, expand_weight, reduce_weight, filter_taps, filter_offset, step_bias, decay_rate, skip_gain, norm_gain, gate_gain, cotangent):
    group = math.gcd(BATCH, max(1, 4096 // LENGTH))
    weights = tuple((item.astype(jnp.float32) for item in (expand_weight, reduce_weight, filter_taps, filter_offset, step_bias, decay_rate, skip_gain, norm_gain, gate_gain)))
    seg_groups = segments.reshape(BATCH // group, group, LENGTH)

    def forward(token_values, layer_weights):
        stacked = token_values.reshape(BATCH // group, group, LENGTH, D)

        def group_pass(carry, item):
            resid, segment = item
            for layer_index in range(LAYERS):
                resid = mixer_layer(resid, segment, *[weight[layer_index] for weight in layer_weights])
            return (carry, resid)
        _, result = lax.scan(jax.checkpoint(group_pass), jnp.zeros((), jnp.float32), (stacked, seg_groups))
        return result.reshape(BATCH, LENGTH, D)
    output, pullback = jax.vjp(forward, tokens.astype(jnp.float32), weights)
    token_grad, weight_grads = pullback(cotangent.astype(jnp.float32))
    return (output.astype(jnp.bfloat16), token_grad.astype(jnp.bfloat16), weight_grads[0], weight_grads[1], weight_grads[2], weight_grads[3], weight_grads[4], weight_grads[5], weight_grads[6], weight_grads[7], weight_grads[8])
```

```python
import functools

import jax
import jax.numpy as jnp
from jax import lax
from jax.experimental import pallas as pl
from jax.experimental.pallas import tpu as pltpu
from jax.sharding import Mesh, PartitionSpec as P

H = 32
P_SIZE = 64
N = 128
CONV = 4
LAYERS = 2
DI = 2048
CH = 2304
D = 1024
EPSILON = 1e-05
Q = 128
LANES = 128
PAIRS = DI // LANES
BLOCKS = CH // LANES
KEYS, READS, KEYS_REST, READS_REST = (slice(DI + i * N, DI + (i + 1) * N) for i in range(4))
ACT = DI + 4 * N
FAR = -1e30
F32 = jnp.float32
BF16 = jnp.bfloat16
VMEM_LIMIT = 56 * 1024 * 1024


def dot_nn(a, b):
    return lax.dot_general(a, b, (((1,), (0,)), ((), ())), preferred_element_type=F32)


def dot_nt(a, b):
    return lax.dot_general(a, b, (((1,), (1,)), ((), ())), preferred_element_type=F32)


def dot_tn(a, b):
    return lax.dot_general(a, b, (((0,), (0,)), ((), ())), preferred_element_type=F32)


def dot_full(a, b):
    return lax.dot_general(
        a, b, (((1,), (0,)), ((), ())), precision=lax.Precision.HIGHEST, preferred_element_type=F32
    )


def two_parts(x):
    high = x.astype(BF16)
    return high, (x - high.astype(F32)).astype(BF16)


def low_lanes():
    return lax.broadcasted_iota(jnp.int32, (Q, LANES), 1) < P_SIZE


def spread(table, first, pair, low):
    a = table[:, first + 2 * pair : first + 2 * pair + 1]
    b = table[:, first + 2 * pair + 1 : first + 2 * pair + 2]
    return jnp.where(low, a, b)


def column(table, index):
    return table[:, index : index + 1]


def lanes_of(index):
    return pl.ds(index * LANES, LANES)


def fold_rows(x):
    return jnp.sum(x.reshape(x.shape[0] // 8, 8, x.shape[1]), axis=0)


STEP, LOGS, TO_END, FROM_START = 0, 32, 64, 96


def front_kernel(
    u_ref, s_ref, rim_ref, segx_ref, taps_ref, heads_ref, oht_ref,
    act_ref, slope_ref, aux_ref, lt_ref, drow_ref, sout_ref, msg_ref,
    ubuf, state, decay, xbuf,
):
    c = pl.program_id(0)

    @pl.when(c == 0)
    def _():
        ubuf[0:8, :] = rim_ref[...].astype(F32)
        state[...] = jnp.zeros_like(state)
        decay[...] = jnp.ones_like(decay)

    @pl.when(c > 0)
    def _():
        ubuf[0:8, :] = ubuf[Q : Q + 8, :]

    seg_rows = segx_ref[pl.ds(pl.multiple_of(c * Q, Q), Q + 8), :]
    seg = seg_rows[8:]
    masks = [(seg_rows[5 + k : 5 + k + Q] == seg).astype(F32) for k in range(CONV - 1)]
    for j in range(BLOCKS):
        cols = lanes_of(j)
        ubuf[8 : 8 + Q, cols] = u_ref[:, cols].astype(F32)
        filtered = taps_ref[4:5, cols] + taps_ref[3:4, cols] * ubuf[8 : 8 + Q, cols]
        for k in range(CONV - 1):
            filtered += taps_ref[k : k + 1, cols] * (ubuf[5 + k : 5 + k + Q, cols] * masks[k])
        gate = 1.0 / (1.0 + jnp.exp(-filtered))
        active = filtered * gate
        act_ref[:, cols] = active.astype(BF16)
        if j >= PAIRS:
            act_ref[:, lanes_of(j + 2)] = two_parts(active)[1]
        slope_ref[:, cols] = (gate * (1.0 + filtered - active)).astype(BF16)

    raw = s_ref[...].astype(F32) + heads_ref[0:1, :]
    step = jnp.maximum(raw, 0.0) + jnp.log1p(jnp.exp(-jnp.abs(raw)))
    rows = lax.broadcasted_iota(jnp.int32, (Q, Q), 0)
    lane = lax.broadcasted_iota(jnp.int32, (Q, Q), 1)
    logs = dot_full((rows >= lane).astype(F32), -(step * heads_ref[1:2, :]))
    last = logs[Q - 1 : Q, :]
    joined = (seg_rows[8:9] == seg_rows[7:8]).astype(F32)
    to_end = jnp.exp(last - logs) * (seg == seg[Q - 1 : Q]).astype(F32)
    from_start = jnp.exp(logs) * (joined * (seg == seg[0:1]).astype(F32))
    aux = jnp.where(
        lane < 64, jnp.where(lane < 32, step, logs), jnp.where(lane < 96, to_end, from_start)
    )
    aux_ref[...] = aux
    lt_ref[0] = logs.T[:H, :]
    through = jnp.exp(last) * joined * (seg[Q - 1 : Q] == seg[0:1]).astype(F32)
    before = decay[0:1, :]
    after = before * through
    row16 = lax.broadcasted_iota(jnp.int32, (16, LANES), 0)
    table = jnp.where(row16 == 0, through, jnp.where(row16 == 1, before, after))
    high, rest = two_parts(table)
    drow = dot_nn(high, oht_ref[...]) + dot_nn(rest, oht_ref[...])
    drow_ref[0] = drow[0:8]
    decay[...] = jnp.broadcast_to(after, decay.shape)

    low = low_lanes()
    for j in range(PAIRS):
        scaled = (spread(aux, STEP, j, low) * act_ref[:, lanes_of(j)].astype(F32)).astype(BF16)
        xbuf[:, lanes_of(j)] = (spread(aux, TO_END, j, low) * scaled.astype(F32)).astype(BF16)
    keys = act_ref[:, KEYS].astype(F32).T.astype(BF16)
    held = state[...] * drow[0:1, :] + dot_nn(keys, xbuf[...])
    state[...] = held
    sout_ref[0] = held
    msg_ref[0:N, :] = held
    msg_ref[N : N + 8, :] = jnp.broadcast_to(drow[2:3], (8, DI))


def within_kernel(act_ref, aux_ref, lt_ref, segx_ref, segr_ref, sprev_ref, skip_ref, y_ref):
    c = pl.program_id(0)
    seg = segx_ref[pl.ds(pl.multiple_of(c * Q + 8, 8), Q), :]
    rows = lax.broadcasted_iota(jnp.int32, (Q, Q), 0)
    lane = lax.broadcasted_iota(jnp.int32, (Q, Q), 1)
    bias = jnp.where((rows >= lane) & (seg == segr_ref[0, 0:1, :]), 0.0, FAR)
    reads = act_ref[:, READS]
    reads_both = jnp.concatenate([reads, act_ref[:, READS_REST]], axis=1)
    keys_twice = jnp.concatenate([act_ref[:, KEYS]] * 2, axis=1)
    scores = dot_nt(reads_both, keys_twice) + dot_nt(reads, act_ref[:, KEYS_REST])
    aux = aux_ref[...]
    low = low_lanes()
    has_prev = (c > 0).astype(F32)
    for j in range(PAIRS):
        cols = lanes_of(j)
        weights = [
            (jnp.exp(column(aux, LOGS + h) - lt_ref[0, h : h + 1, :] + bias) * scores).astype(BF16)
            for h in (2 * j, 2 * j + 1)
        ]
        values = act_ref[:, cols].astype(F32)
        scaled = spread(aux, STEP, j, low) * values
        stack = jnp.concatenate(
            [jnp.where(low, scaled, 0.0), jnp.where(low, 0.0, scaled)], axis=0
        ).astype(BF16)
        high, rest = two_parts(sprev_ref[0, :, cols])
        carried = dot_nn(reads_both, jnp.concatenate([high, high], axis=0)) + dot_nn(reads, rest)
        carried *= spread(aux, FROM_START, j, low) * has_prev
        y_ref[:, cols] = (
            dot_nn(jnp.concatenate(weights, axis=1), stack)
            + carried
            + skip_ref[0:1, cols] * values
        )


def gate_kernel(
    yloc_ref, aux_ref, drow_ref, sin_ref, reads_ref, rest_ref, z_ref, gain_ref, y_ref, out_ref, gbuf
):
    aux = aux_ref[...]
    reads = reads_ref[...]
    reads_both = jnp.concatenate([reads, rest_ref[...]], axis=1)
    low = low_lanes()
    total = jnp.zeros((Q, LANES), F32)
    for j in range(PAIRS):
        cols = lanes_of(j)
        high, rest = two_parts(sin_ref[:, cols])
        carried = dot_nn(reads_both, jnp.concatenate([high, high], axis=0)) + dot_nn(reads, rest)
        y = yloc_ref[:, cols] + carried * (spread(aux, FROM_START, j, low) * drow_ref[0, 1:2, cols])
        y_ref[:, cols] = y
        z = z_ref[:, cols].astype(F32)
        gated = y * (z / (1.0 + jnp.exp(-z)))
        gbuf[:, cols] = gated
        total += gated * gated
    scale = lax.rsqrt(jnp.sum(total, axis=1, keepdims=True) * (1.0 / DI) + EPSILON)
    for j in range(PAIRS):
        cols = lanes_of(j)
        out_ref[:, cols] = (gbuf[:, cols] * scale * gain_ref[0:1, cols]).astype(BF16)


def gate_back_kernel(
    dout_ref, y_ref, z_ref, gain_ref, reads_ref, aux_ref, drow_ref,
    dy_ref, rest_ref, dz_ref, ggrad_ref, zloc_ref, gmsg_ref, dsuf_ref,
    gbuf, grad_state, suffix, xbuf,
):
    @pl.when(pl.program_id(0) == 0)
    def _():
        ggrad_ref[...] = jnp.zeros_like(ggrad_ref)
        grad_state[...] = jnp.zeros_like(grad_state)
        suffix[...] = jnp.ones_like(suffix)

    aux = aux_ref[...]
    low = low_lanes()
    total = jnp.zeros((Q, LANES), F32)
    cross = jnp.zeros((Q, LANES), F32)
    for j in range(PAIRS):
        cols = lanes_of(j)
        z = z_ref[:, cols].astype(F32)
        gated = y_ref[:, cols] * (z / (1.0 + jnp.exp(-z)))
        gbuf[:, cols] = gated
        total += gated * gated
        cross += gated * (dout_ref[:, cols] * gain_ref[0:1, cols])
    scale = lax.rsqrt(jnp.sum(total, axis=1, keepdims=True) * (1.0 / DI) + EPSILON)
    pull = jnp.sum(cross, axis=1, keepdims=True) * (scale * scale * scale * (1.0 / DI))
    scale = jnp.broadcast_to(scale, (Q, LANES))
    pull = jnp.broadcast_to(pull, (Q, LANES))
    for j in range(PAIRS):
        cols = lanes_of(j)
        z = z_ref[:, cols].astype(F32)
        gate = 1.0 / (1.0 + jnp.exp(-z))
        gated = gbuf[:, cols]
        scaled = dout_ref[:, cols] * scale
        ggrad_ref[:, cols] += fold_rows(scaled * gated)
        d_gated = scaled * gain_ref[0:1, cols] - gated * pull
        dy, rest = two_parts(d_gated * (z * gate))
        dy_ref[:, cols] = dy
        rest_ref[:, cols] = rest
        dz_ref[:, cols] = (d_gated * y_ref[:, cols] * (gate * (1.0 + z * (1.0 - gate)))).astype(BF16)
        xbuf[:, cols] = (dy.astype(F32) * spread(aux, FROM_START, j, low)).astype(BF16)
    zloc_ref[0] = grad_state[...].astype(BF16)
    dsuf_ref[0] = suffix[...]
    reads = reads_ref[...].astype(F32).T.astype(BF16)
    through = drow_ref[0, 0:1, :]
    grad_state[...] = grad_state[...] * through + dot_nn(reads, xbuf[...])
    suffix[...] = suffix[...] * through
    gmsg_ref[...] = grad_state[...].astype(BF16)


def within_back_kernel(
    act_ref, aux_ref, lt_ref, segx_ref, segr_ref, dy_ref, rest_ref, sprev_ref, drow_ref, sin_ref, zloc_ref,
    dxs_ref, dbc_ref, wbuf, wrest, ibuf, irest, ebuf,
):
    c = pl.program_id(0)
    seg = segx_ref[pl.ds(pl.multiple_of(c * Q + 8, 8), Q), :]
    rows = lax.broadcasted_iota(jnp.int32, (Q, Q), 0)
    lane = lax.broadcasted_iota(jnp.int32, (Q, Q), 1)
    bias = jnp.where((rows <= lane) & (seg == segr_ref[0, 0:1, :]), 0.0, FAR)
    keys, reads = act_ref[:, KEYS], act_ref[:, READS]
    scores = dot_nt(
        jnp.concatenate([keys, keys], axis=1), jnp.concatenate([reads, act_ref[:, READS_REST]], axis=1)
    ) + dot_nt(act_ref[:, KEYS_REST], reads)
    aux = aux_ref[...]
    low = low_lanes()
    has_prev = (c > 0).astype(F32)
    d_scores = jnp.zeros((Q, Q), F32)
    for j in range(PAIRS):
        cols = lanes_of(j)
        fades = [
            jnp.exp(lt_ref[0, h : h + 1, :] - column(aux, LOGS + h) + bias)
            for h in (2 * j, 2 * j + 1)
        ]
        weights = jnp.concatenate([(fade * scores).astype(BF16) for fade in fades], axis=1)
        dy = dy_ref[:, cols]
        dy_wide = dy.astype(F32)
        dy_rest = rest_ref[:, cols]
        stack = jnp.concatenate(
            [jnp.where(low, dy_wide, 0.0), jnp.where(low, 0.0, dy_wide)], axis=0
        ).astype(BF16)
        scaled = (spread(aux, STEP, j, low) * act_ref[:, cols].astype(F32)).astype(BF16).astype(F32)
        both = jnp.concatenate(
            [jnp.where(low, scaled, 0.0), jnp.where(low, 0.0, scaled)], axis=0
        ).astype(BF16)
        d_weights = dot_nt(
            jnp.concatenate([both, both], axis=1), jnp.concatenate([dy, dy_rest], axis=1)
        )
        d_scores += d_weights[:Q] * fades[0] + d_weights[Q:] * fades[1]
        to_end = spread(aux, TO_END, j, low)
        dxs_ref[:, cols] = dot_nn(weights, stack) + to_end * dot_nn(keys, zloc_ref[0, :, cols])
        wbuf[:, cols], wrest[:, cols] = two_parts(
            (dy_wide + dy_rest.astype(F32)) * spread(aux, FROM_START, j, low)
        )
        ebuf[:, cols] = (to_end * scaled).astype(BF16)
        ibuf[:, cols], irest[:, cols] = two_parts(
            drow_ref[0, 1:2, cols] * sin_ref[:, cols] + has_prev * sprev_ref[0, :, cols]
        )
    dbc_ref[:, 0:N] = dot_nn(d_scores.astype(BF16), reads) + dot_nt(ebuf[...], zloc_ref[0])
    high, rest = two_parts(d_scores.T)
    dbc_ref[:, N:] = (
        dot_nn(high, keys)
        + dot_nn(rest, keys)
        + dot_nt(wbuf[...], ibuf[...])
        + dot_nt(wrest[...], ibuf[...])
        + dot_nt(wbuf[...], irest[...])
    )


def last_kernel(
    act_ref, aux_ref, slope_ref, u_ref, s_ref, rim_ref, segx_ref, taps_ref, heads_ref, skip_ref,
    oh_ref, dy_ref, y_ref, dxs_ref, dbc_ref, sout_ref, drow_ref, sin_ref, zloc_ref, dsuf_ref, zdev_ref,
    du_ref, ds_ref, tail_ref, rimout_ref, tgrad_ref, hgrad_ref,
    dbuf, qhigh, qrest, vhigh, vrest, ebuf, sums, skips,
):
    i = pl.program_id(0)
    count = pl.num_programs(0)
    c = count - 1 - i

    @pl.when(i == 0)
    def _():
        dbuf[Q : Q + 8, :] = jnp.zeros((8, CH), F32)
        tgrad_ref[...] = jnp.zeros_like(tgrad_ref)
        hgrad_ref[...] = jnp.zeros_like(hgrad_ref)
        skips[...] = jnp.zeros_like(skips)

    @pl.when(i > 0)
    def _():
        dbuf[Q : Q + 8, :] = dbuf[0:8, :]

    aux = aux_ref[...]
    low = low_lanes()
    keys = act_ref[:, KEYS]
    for j in range(PAIRS):
        cols = lanes_of(j)
        dy = dy_ref[:, cols].astype(F32)
        values = act_ref[:, cols].astype(F32)
        step = spread(aux, STEP, j, low)
        scaled = (step * values).astype(BF16).astype(F32)
        reach = spread(aux, TO_END, j, low) * dsuf_ref[0, 0:1, cols]
        dxs = dxs_ref[:, cols] + reach * dot_nn(keys, zdev_ref[:, cols])
        ebuf[:, cols] = (reach * scaled).astype(BF16)
        skip = skip_ref[0:1, cols]
        dbuf[0:Q, cols] = (step * dxs + skip * dy) * slope_ref[:, cols].astype(F32)
        qhigh[:, cols], qrest[:, cols] = two_parts(dy * (y_ref[:, cols] - skip * values) - scaled * dxs)
        vhigh[:, cols], vrest[:, cols] = two_parts(values * dxs)
        skips[:, cols] += fold_rows(values * dy)
        arrived = zloc_ref[0, :, cols].astype(F32) + dsuf_ref[0, 0:1, cols] * zdev_ref[:, cols].astype(F32)
        leaving = sout_ref[0, :, cols] + drow_ref[0, 2:3, cols] * sin_ref[:, cols]
        sums[:, cols] = fold_rows(arrived * leaving)
    d_keys = dbc_ref[:, 0:N] + dot_nt(ebuf[...], zdev_ref[...])
    dbuf[0:Q, DI : DI + N] = d_keys * slope_ref[:, DI : DI + N].astype(F32)
    dbuf[0:Q, DI + N :] = dbc_ref[:, N:] * slope_ref[:, DI + N :].astype(F32)

    hot = oh_ref[...]

    def by_head(x):
        high, rest = two_parts(x)
        return dot_nn(high, hot) + dot_nn(rest, hot)

    d_logs = dot_nn(qhigh[...], hot) + dot_nn(qrest[...], hot)
    d_last = jnp.sum(by_head(sums[...]), axis=0, keepdims=True)
    rows = lax.broadcasted_iota(jnp.int32, (Q, Q), 0)
    lane = lax.broadcasted_iota(jnp.int32, (Q, Q), 1)
    d_decay = dot_full((rows <= lane).astype(F32), d_logs) + d_last
    raw = s_ref[...].astype(F32) + heads_ref[0:1, :]
    step = jnp.maximum(raw, 0.0) + jnp.log1p(jnp.exp(-jnp.abs(raw)))
    d_step = dot_nn(vhigh[...], hot) + dot_nn(vrest[...], hot) - heads_ref[1:2, :] * d_decay
    d_raw = d_step / (1.0 + jnp.exp(-raw))
    ds_ref[...] = d_raw.astype(BF16)
    hgrad_ref[0:8, :] += fold_rows(d_raw)
    hgrad_ref[8:16, :] += fold_rows(-(step * d_decay))

    @pl.when(i == count - 1)
    def _():
        hgrad_ref[16:24, :] = by_head(skips[...])

    seg_rows = segx_ref[pl.ds(pl.multiple_of(c * Q + 8, 8), Q + 8), :]
    seg = seg_rows[:Q]
    masks = [(seg_rows[m : m + Q] == seg).astype(F32) for m in range(1, CONV)]
    for j in range(BLOCKS):
        cols = lanes_of(j)
        d_filtered = dbuf[0:Q, cols]
        u = u_ref[:, cols].astype(F32)
        du = taps_ref[3:4, cols] * d_filtered
        tgrad_ref[24:32, cols] += fold_rows(u * d_filtered)
        tgrad_ref[32:40, cols] += fold_rows(d_filtered)
        for m in range(1, CONV):
            later = dbuf[m : m + Q, cols] * masks[m - 1]
            du += taps_ref[3 - m : 4 - m, cols] * later
            tgrad_ref[8 * (3 - m) : 8 * (4 - m), cols] += fold_rows(u * later)
        du_ref[:, cols] = du.astype(BF16)

        @pl.when(i == 0)
        def _():
            tail_ref[:, cols] = du[Q - 8 :]

    @pl.when(i == count - 1)
    def _():
        near = segx_ref[0:16, :]
        rim_masks = [(near[m : m + 8] == near[0:8]).astype(F32) for m in range(1, CONV)]
        for j in range(BLOCKS):
            cols = lanes_of(j)
            edge = jnp.concatenate([jnp.zeros((8, LANES), F32), dbuf[0:8, cols]], axis=0)
            u = rim_ref[:, cols].astype(F32)
            out = jnp.zeros((8, LANES), F32)
            for m in range(1, CONV):
                later = edge[m : m + 8] * rim_masks[m - 1]
                out += taps_ref[3 - m : 4 - m, cols] * later
                tgrad_ref[8 * (3 - m) : 8 * (4 - m), cols] += u * later
            rimout_ref[:, cols] = out.astype(BF16)


def whole(shape):
    return pl.BlockSpec(shape, lambda i: (0,) * len(shape))


def by_rows(shape, count=None):
    if count is None:
        return pl.BlockSpec(shape, lambda i: (i,) + (0,) * (len(shape) - 1))
    return pl.BlockSpec(shape, lambda i: (count - 1 - i,) + (0,) * (len(shape) - 1))


def struct(shape, dtype):
    return jax.ShapeDtypeStruct(shape, dtype)


def call(kernel, grid, in_specs, out_specs, out_shape, scratch, flops, moved, name):
    return pl.pallas_call(
        kernel,
        grid=(grid,),
        in_specs=in_specs,
        out_specs=out_specs,
        out_shape=out_shape,
        scratch_shapes=scratch,
        compiler_params=pltpu.CompilerParams(
            dimension_semantics=("arbitrary",), vmem_limit_bytes=VMEM_LIMIT
        ),
        cost_estimate=pl.CostEstimate(flops=flops, bytes_accessed=moved, transcendentals=0),
        name=name,
    )


MIB = 1 << 20


def ssd_front(u, s4, rim, segx, taps, heads, oht):
    T = u.shape[0]
    nc = T // Q
    return call(
        front_kernel, nc,
        [by_rows((Q, CH)), by_rows((Q, LANES)), whole((8, CH)), whole(segx.shape), whole(taps.shape),
         whole(heads.shape), whole(oht.shape)],
        [by_rows((Q, ACT)), by_rows((Q, CH)), by_rows((Q, LANES)), by_rows((1, H, Q)),
         by_rows((1, 8, DI)), by_rows((1, N, DI)), whole((N + 8, DI))],
        [struct((T, ACT), BF16), struct((T, CH), BF16), struct((T, LANES), F32), struct((nc, H, Q), F32),
         struct((nc, 8, DI), F32), struct((nc, N, DI), F32), struct((N + 8, DI), F32)],
        [pltpu.VMEM((Q + 8, CH), F32), pltpu.VMEM((N, DI), F32), pltpu.VMEM((8, LANES), F32),
         pltpu.VMEM((Q, DI), BF16)],
        2_000_000_000, 12 * MIB, "ssd_front",
    )(u, s4, rim, segx, taps, heads, oht)


def previous(shape):
    return pl.BlockSpec(shape, lambda i: (jnp.maximum(i - 1, 0), 0, 0))


def ssd_within(act, aux, lt, segx, segr, sout, skip):
    T = act.shape[0]
    nc = T // Q
    return call(
        within_kernel, nc,
        [by_rows((Q, ACT)), by_rows((Q, LANES)), by_rows((1, H, Q)), whole(segx.shape),
         by_rows((1, 8, LANES)), previous((1, N, DI)), whole(skip.shape)],
        by_rows((Q, DI)), struct((T, DI), F32), [],
        4_000_000_000, 10 * MIB, "ssd_within",
    )(act, aux, lt, segx, segr, sout, skip)


def ssd_gate(yloc, aux, drow, s_in, act, z, gain):
    T = yloc.shape[0]
    nc = T // Q
    reads = pl.BlockSpec((Q, N), lambda i: (i, READS.start // N))
    rest = pl.BlockSpec((Q, N), lambda i: (i, READS_REST.start // N))
    return call(
        gate_kernel, nc,
        [by_rows((Q, DI)), by_rows((Q, LANES)), by_rows((1, 8, DI)), whole((N, DI)), reads,
         rest, by_rows((Q, DI)), whole(gain.shape)],
        [by_rows((Q, DI)), by_rows((Q, DI))],
        [struct((T, DI), F32), struct((T, DI), BF16)],
        [pltpu.VMEM((Q, DI), F32)],
        2_000_000_000, 14 * MIB, "ssd_gate",
    )(yloc, aux, drow, s_in, act, act, z, gain)


def gate_back(dout, y, z, gain, act, aux, drow):
    T = y.shape[0]
    nc = T // Q
    reads = pl.BlockSpec((Q, N), lambda i: (nc - 1 - i, READS.start // N))
    return call(
        gate_back_kernel, nc,
        [by_rows((Q, DI), nc), by_rows((Q, DI), nc), by_rows((Q, DI), nc), whole(gain.shape), reads,
         by_rows((Q, LANES), nc), by_rows((1, 8, DI), nc)],
        [by_rows((Q, DI), nc)] * 3 + [whole((8, DI)), by_rows((1, N, DI), nc),
         whole((N, DI)), by_rows((1, 8, DI), nc)],
        [struct((T, DI), BF16)] * 3 + [struct((8, DI), F32), struct((nc, N, DI), BF16),
         struct((N, DI), BF16), struct((nc, 8, DI), F32)],
        [pltpu.VMEM((Q, DI), F32), pltpu.VMEM((N, DI), F32), pltpu.VMEM((8, DI), F32),
         pltpu.VMEM((Q, DI), BF16)],
        3_000_000_000, 18 * MIB, "gate_back",
    )(dout, y, z, gain, act, aux, drow)


def within_back(act, aux, lt, segx, segr, dy, rest, sout, drow, s_in, zloc):
    T = act.shape[0]
    nc = T // Q
    return call(
        within_back_kernel, nc,
        [by_rows((Q, ACT)), by_rows((Q, LANES)), by_rows((1, H, Q)), whole(segx.shape),
         by_rows((1, 8, LANES)), by_rows((Q, DI)), by_rows((Q, DI)), previous((1, N, DI)), by_rows((1, 8, DI)),
         whole((N, DI)), by_rows((1, N, DI))],
        [by_rows((Q, DI)), by_rows((Q, 2 * N))],
        [struct((T, DI), F32), struct((T, 2 * N), F32)],
        [pltpu.VMEM((Q, DI), BF16)] * 5,
        8_000_000_000, 16 * MIB, "within_back",
    )(act, aux, lt, segx, segr, dy, rest, sout, drow, s_in, zloc)


def ssd_last(act, aux, slope, u, s4, rim, segx, taps, heads, skip, oh, dy, y, dxs, dbc, sout, drow, s_in,
             zloc, dsuf, zdev):
    T = act.shape[0]
    nc = T // Q
    return call(
        last_kernel, nc,
        [by_rows((Q, ACT), nc), by_rows((Q, LANES), nc), by_rows((Q, CH), nc), by_rows((Q, CH), nc),
         by_rows((Q, LANES), nc), whole((8, CH)), whole(segx.shape), whole(taps.shape),
         whole(heads.shape), whole(skip.shape), whole(oh.shape), by_rows((Q, DI), nc),
         by_rows((Q, DI), nc), by_rows((Q, DI), nc), by_rows((Q, 2 * N), nc), by_rows((1, N, DI), nc),
         by_rows((1, 8, DI), nc), whole((N, DI)), by_rows((1, N, DI), nc), by_rows((1, 8, DI), nc),
         whole((N, DI))],
        [by_rows((Q, CH), nc), by_rows((Q, LANES), nc), whole((8, CH)), whole((8, CH)), whole((40, CH)),
         whole((24, LANES))],
        [struct((T, CH), BF16), struct((T, LANES), BF16), struct((8, CH), F32), struct((8, CH), BF16),
         struct((40, CH), F32), struct((24, LANES), F32)],
        [pltpu.VMEM((Q + 8, CH), F32), pltpu.VMEM((Q, DI), BF16), pltpu.VMEM((Q, DI), BF16),
         pltpu.VMEM((Q, DI), BF16), pltpu.VMEM((Q, DI), BF16), pltpu.VMEM((Q, DI), BF16),
         pltpu.VMEM((8, DI), F32), pltpu.VMEM((8, DI), F32)],
        6_000_000_000, 24 * MIB, "ssd_last",
    )(act, aux, slope, u, s4, rim, segx, taps, heads, skip, oh, dy, y, dxs, dbc, sout, drow, s_in,
      zloc, dsuf, zdev)


def swap(value, axis):
    return lax.ppermute(value, axis, [(0, 1), (1, 0)])


def flip(value, axis, bit):
    size = lax.axis_size(axis)
    return lax.ppermute(value, axis, [(i, i ^ bit) for i in range(size)])


def ordered(index, mine, other, axis):
    return jnp.where(
        index == 0, jnp.concatenate([mine, other], axis), jnp.concatenate([other, mine], axis)
    )


CTX = ("zz", "core")


def routes():
    n = lax.axis_size("zz") * lax.axis_size("core")
    half = n // 2
    first = [(i, i // 2 + (half if i % 2 else 0)) for i in range(n)]
    second = [(i, i // 2 + (0 if i % 2 else half)) for i in range(n)]
    return half, first, second


def gather_tokens(x):
    half, first, second = routes()
    me = lax.axis_index(CTX)
    even = me % 2 == 0
    a = lax.ppermute(jnp.where(even, x[0], x[1]), CTX, first)
    b = lax.ppermute(jnp.where(even, x[1], x[0]), CTX, second)
    early = me < half
    return jnp.concatenate([jnp.where(early, a, b), jnp.where(early, b, a)], axis=0)


def scatter_tokens(x):
    half, first, second = routes()
    me = lax.axis_index(CTX)
    early = me < half
    rows = x.shape[0] // 2
    x0, x1 = x[:rows], x[rows:]
    a = lax.ppermute(jnp.where(early, x0, x1), CTX, [(d, s) for s, d in first])
    b = lax.ppermute(jnp.where(early, x1, x0), CTX, [(d, s) for s, d in second])
    even = me % 2 == 0
    return jnp.stack([jnp.where(even, a, b), jnp.where(even, b, a)])


def next_piece(value, backward=False):
    n = lax.axis_size("zz") * lax.axis_size("core")
    half = n // 2
    pairs = [(i, i + 1) for i in range(n - 1) if i + 1 != half]
    if backward:
        pairs = [(d, s) for s, d in pairs]
    return lax.ppermute(value, CTX, pairs)


def after(value, earlier):
    value, _ = lax.optimization_barrier((value, earlier))
    return value


def fetch_peer(own, core, earlier=None):
    rows = own.shape[0] // 2
    part = lax.dynamic_slice_in_dim(own, core * rows, rows, 0)
    if earlier is not None:
        part = after(part, earlier)
    got = swap(part, "fsdp")
    return ordered(core, got, swap(got, "core"), 0), got


def carry_forward(core, msg):
    other = swap(msg, "core")

    s_mine, d_mine = msg[:N], msg[N : N + 1]
    s_other, d_other = other[:N], other[N : N + 1]
    lead = core == 0
    s_first, d_first = jnp.where(lead, s_mine, s_other), jnp.where(lead, d_mine, d_other)
    s_second, d_second = jnp.where(lead, s_other, s_mine), jnp.where(lead, d_other, d_mine)
    total = d_second * s_first + s_second
    through = d_first * d_second
    chips = lax.axis_size("zz") // 2
    total = halves(total, core, 0)[0]
    prefix = jnp.zeros_like(total)
    for hop in range(1, chips):
        sent = total if hop == 1 else through * prefix + total
        pairs = [(hop - 1, hop), (chips + hop - 1, chips + hop)]
        prefix = prefix + lax.ppermute(sent, "zz", pairs)
    prefix = ordered(core, prefix, swap(prefix, "core"), 0)
    incoming = jnp.where(lead, prefix, d_first * prefix + s_first)
    return incoming, (d_first, d_second)


def carry_backward(core, msg, decays):
    other = swap(msg, "core")
    d_first, d_second = decays
    lead = core == 0
    g_first = jnp.where(lead, msg, other).astype(F32)
    g_second = jnp.where(lead, other, msg).astype(F32)
    total = g_first + d_first * g_second
    through = d_first * d_second
    chips = lax.axis_size("zz") // 2
    suffix = jnp.zeros_like(total)
    for hop in range(1, chips):
        sent = total if hop == 1 else through * suffix + total
        pairs = [(chips - hop, chips - hop - 1), (2 * chips - hop, 2 * chips - hop - 1)]
        suffix = suffix + lax.ppermute(sent.astype(BF16), "zz", pairs).astype(F32)
    arriving = jnp.where(lead, g_second + d_second * suffix, suffix)
    return arriving.astype(BF16)


def rms_parts(values):
    return lax.rsqrt(jnp.mean(values * values, axis=-1, keepdims=True) + EPSILON)


def halves(array, index, axis):
    size = array.shape[axis] // 2
    mine = lax.dynamic_slice_in_dim(array, index * size, size, axis)
    other = lax.dynamic_slice_in_dim(array, (1 - index) * size, size, axis)
    return mine, other


def levels():
    out = [("rep", 1)]
    bit = 1
    while bit < lax.axis_size("zz"):
        out.append(("zz", bit))
        bit *= 2
    return out


def sum_shards(partial, fsdp):
    mine, other = halves(partial, fsdp, 0)
    total = mine + swap(other.astype(BF16), "fsdp").astype(F32)
    steps = levels()
    for axis, bit in steps:
        which = (lax.axis_index(axis) // bit) % 2
        mine, other = halves(total, which, 0)
        total = mine + flip(other.astype(BF16), axis, bit).astype(F32)
    total = total.astype(BF16)
    for axis, bit in reversed(steps):
        which = (lax.axis_index(axis) // bit) % 2
        total = ordered(which, total, flip(total, axis, bit), 0)
    return total


def sum_small(packed):
    packed = packed + swap(packed, "core")
    packed = packed + swap(packed, "fsdp")
    for axis, bit in levels():
        packed = packed + flip(packed, axis, bit)
    return packed


def local(
    tokens,
    segments,
    expand_weight,
    reduce_weight,
    filter_taps,
    filter_offset,
    step_bias,
    decay_rate,
    skip_gain,
    norm_gain,
    gate_gain,
    cotangent,
):
    rows = tokens.shape[1]
    T = 2 * rows
    fsdp = lax.axis_index("fsdp")
    core = lax.axis_index("core")
    me = lax.axis_index(CTX)
    n = lax.axis_size("zz") * lax.axis_size("core")
    half = n // 2

    def pad(x, width):
        return jnp.pad(x, ((0, 0), (0, 0), (0, width - x.shape[-1])))

    heads_packed = jnp.concatenate([step_bias, decay_rate, skip_gain], axis=-1)
    own = jnp.concatenate(
        [filter_taps, filter_offset[:, None], pad(norm_gain[:, None], CH // 2),
         pad(gate_gain[:, None], CH // 2), pad(heads_packed[:, None], CH // 2)], axis=1
    )
    other = swap(own, "fsdp")
    lead = fsdp == 0
    low_half = jnp.where(lead, own, other).astype(F32)
    high_half = jnp.where(lead, other, own).astype(F32)

    def joined(row, start, size):
        return jnp.concatenate(
            [low_half[:, row, start : start + size], high_half[:, row, start : start + size]], axis=-1
        )

    taps_all = jnp.concatenate([low_half[:, :5], high_half[:, :5]], axis=-1)
    taps_all = jnp.pad(taps_all, ((0, 0), (0, 3), (0, 0)))
    norm_all, gate_all = joined(5, 0, D // 2), joined(6, 0, DI // 2)
    bias_all, rate_all, skip_all = joined(7, 0, H // 2), joined(7, H // 2, H // 2), joined(7, H, H // 2)
    heads_all = jnp.pad(
        jnp.stack([jnp.tile(bias_all, (1, 4)), jnp.tile(rate_all, (1, 4))], axis=1), ((0, 0), (0, 6), (0, 0))
    )
    skip_rows = jnp.repeat(skip_all, P_SIZE, axis=-1)

    hot = (
        lax.broadcasted_iota(jnp.int32, (DI, LANES), 0) // P_SIZE
        == lax.broadcasted_iota(jnp.int32, (DI, LANES), 1)
    ).astype(BF16)
    hot_t = (
        lax.broadcasted_iota(jnp.int32, (LANES, DI), 1) // P_SIZE
        == lax.broadcasted_iota(jnp.int32, (LANES, DI), 0)
    ).astype(BF16)

    seq = (me >= half).astype(jnp.int32)
    padded = jnp.pad(segments, ((0, 0), (8, 8)), constant_values=-1)
    seg_line = lax.dynamic_slice(padded, (seq, (me % half) * T), (1, T + 16))[0].astype(F32)
    segx = jnp.broadcast_to(seg_line[:, None], (T + 16, LANES))
    segr = jnp.broadcast_to(seg_line[8 : 8 + T].reshape(T // Q, 1, Q), (T // Q, 8, Q))

    weights = []
    earlier = None
    for layer in range(LAYERS):
        expand_peer, earlier = fetch_peer(expand_weight[layer], core, earlier)
        reduce_peer, earlier = fetch_peer(reduce_weight[layer], core, earlier)
        weights.append(
            (ordered(fsdp, expand_weight[layer], expand_peer, 0),
             ordered(fsdp, reduce_weight[layer], reduce_peer, 0))
        )

    resid = gather_tokens(tokens).astype(F32)
    saved = []
    for layer in range(LAYERS):
        expand, reduce = weights[layer]
        normed = (resid * rms_parts(resid) * norm_all[layer]).astype(BF16)
        mixed = dot_nn(normed, expand).astype(BF16)
        z, u, s = mixed[:, :DI], mixed[:, DI : DI + CH], mixed[:, DI + CH :]
        s4 = jnp.tile(s, (1, LANES // H))
        rim = next_piece(u[T - 8 :])
        taps, heads = taps_all[layer], heads_all[layer]
        skip = skip_rows[layer][None]
        act, slope, aux, lt, drow, sout, msg = ssd_front(u, s4, rim, segx, taps, heads, hot_t)
        s_in, decays = carry_forward(core, msg)
        yloc = ssd_within(act, aux, lt, segx, segr, sout, skip)
        gain = gate_all[layer][None]
        y, out_in = ssd_gate(yloc, aux, drow, s_in, act, z, gain)
        normed_both = jnp.concatenate([normed, swap(normed, "core")], axis=0)
        out_both = jnp.concatenate([out_in, swap(out_in, "core")], axis=0)
        saved.append((resid, normed_both, z, u, s4, rim, act, slope, aux, lt, drow, sout, s_in, decays, y, out_both))
        resid = resid + dot_nn(out_in, reduce)
    layer_out = scatter_tokens(resid.astype(BF16))

    grad = gather_tokens(cotangent).astype(F32)
    expand_z, expand_u, reduce_g, small = [None] * 2, [None] * 2, [None] * 2, [None] * 2
    for layer in reversed(range(LAYERS)):
        expand, reduce = weights[layer]
        (resid_in, normed_both, z, u, s4, rim, act, slope, aux, lt, drow, sout, s_in, decays, y, out_both) = saved[layer]
        taps, heads = taps_all[layer], heads_all[layer]
        skip = skip_rows[layer][None]
        gain = gate_all[layer][None]
        grad_low = grad.astype(BF16)
        dout = dot_nt(grad_low, reduce)
        low_mine, low_other = halves(grad_low, core, 1)
        low_both = jnp.concatenate([low_mine, swap(low_other, "core")], axis=0)
        reduce_g[layer] = sum_shards(dot_tn(out_both, low_both), fsdp)
        dy, dy_rest, dz, ggrad, zloc, gmsg, dsuf = gate_back(dout, y, z, gain, act, aux, drow)
        zdev = carry_backward(core, gmsg, decays)
        dz_mine, dz_other = halves(dz, core, 1)
        dz_both = jnp.concatenate([dz_mine, swap(dz_other, "core")], axis=0)
        expand_z[layer] = sum_shards(dot_tn(normed_both, dz_both), fsdp)
        dxs, dbc = within_back(act, aux, lt, segx, segr, dy, dy_rest, sout, drow, s_in, zloc)
        du, ds, tail, rimout, tgrad, hgrad = ssd_last(
            act, aux, slope, u, s4, rim, segx, taps, heads, skip, hot, dy, y, dxs, dbc, sout, drow, s_in,
            zloc, dsuf, zdev
        )
        tail = (tail + next_piece(rimout, True).astype(F32)).astype(BF16)
        du = lax.dynamic_update_slice(du, tail, (T - 8, 0))
        ds = ds[:, :H]
        du_mine, du_other = halves(du, core, 1)
        us_both = jnp.concatenate(
            [jnp.concatenate([du_mine, ds], axis=1),
             swap(jnp.concatenate([du_other, ds], axis=1), "core")], axis=0
        )
        expand_u[layer] = sum_shards(dot_tn(normed_both, us_both), fsdp)
        d_mixed = jnp.concatenate([dz, du, ds], axis=1)
        d_normed = dot_nt(d_mixed, expand)
        scale = rms_parts(resid_in)
        unit = resid_in * scale
        pulled = d_normed * norm_all[layer]
        grad = grad + scale * (pulled - unit * jnp.mean(pulled * unit, axis=-1, keepdims=True))
        norm_grad = jnp.sum(d_normed * unit, axis=0)
        tgrad = jnp.sum(tgrad.reshape(5, 8, CH), axis=1).reshape(-1)
        hgrad = jnp.sum(hgrad.reshape(3, 8, LANES), axis=1)[:, :H].reshape(-1)
        small[layer] = jnp.concatenate([tgrad, jnp.sum(ggrad, axis=0), norm_grad, hgrad])

    token_grads = scatter_tokens(grad.astype(BF16))
    size = small[0].shape[0]
    padded_size = -(-size // 1024) * 1024
    packed = jnp.pad(jnp.stack(small), ((0, 0), (0, padded_size - size)))
    packed = sum_small(packed.reshape(-1, LANES)).reshape(LAYERS, padded_size)

    def own_half(x):
        return halves(x, fsdp, x.ndim - 1)[0]

    tap_grads = own_half(packed[:, : 4 * CH].reshape(LAYERS, 4, CH))
    offset_grads = own_half(packed[:, 4 * CH : 5 * CH])
    at = 5 * CH
    gating_grads = own_half(packed[:, at : at + DI])
    at += DI
    norm_grads = own_half(packed[:, at : at + D])
    at += D
    step_grads = own_half(packed[:, at : at + H])
    decay_grads = own_half(packed[:, at + H : at + 2 * H])
    skip_grads = own_half(packed[:, at + 2 * H : at + 3 * H])

    expand_grads, reduce_grads = [], []
    for layer in range(LAYERS):
        zg = ordered(core, expand_z[layer], swap(expand_z[layer], "core"), 1)
        ug = expand_u[layer]
        sg = ug[:, CH // 2 :]
        ug = ug[:, : CH // 2]
        ug = ordered(core, ug, swap(ug, "core"), 1)
        expand_grads.append(jnp.concatenate([zg, ug, sg], axis=1).astype(F32))
        reduce_grads.append(ordered(core, reduce_g[layer], swap(reduce_g[layer], "core"), 1).astype(F32))
    return (
        layer_out,
        token_grads,
        jnp.stack(expand_grads),
        jnp.stack(reduce_grads),
        tap_grads,
        offset_grads,
        step_grads,
        decay_grads,
        skip_grads,
        norm_grads,
        gating_grads,
    )


def solution(mesh):
    rep, fsdp, ctx = (mesh.shape[name] for name in ("rep", "fsdp", "ctx"))
    inner = Mesh(mesh.devices.reshape(rep, fsdp, ctx // 2, 2), ("rep", "fsdp", "zz", "core"))
    tokens = P(("rep", "fsdp"), ("zz", "core"), None)
    first, last = P(None, "fsdp"), P(None, None, "fsdp")
    return jax.shard_map(
        local,
        mesh=inner,
        in_specs=(
            tokens, P(("rep", "fsdp"), None), P(None, "fsdp", None), P(None, "fsdp", None), last,
            first, first, first, first, first, first, tokens,
        ),
        out_specs=(
            tokens, tokens, P(None, "fsdp", None), P(None, "fsdp", None), last,
            first, first, first, first, first, first,
        ),
        check_vma=False,
    )
```

```python
import functools

import jax
import jax.numpy as jnp
from jax import lax
from jax.experimental import pallas as pl
from jax.experimental.pallas import tpu as pltpu
from jax.sharding import Mesh, PartitionSpec as P

H = 32
P_SIZE = 64
N = 128
CONV = 4
LAYERS = 2
DI = 2048
CH = 2304
D = 1024
EPSILON = 1e-05
Q = 128
LANES = 128
PAIRS = DI // LANES
BLOCKS = CH // LANES
KEYS, READS, KEYS_REST, READS_REST = (slice(DI + i * N, DI + (i + 1) * N) for i in range(4))
ACT = DI + 4 * N
E = DI + CH + H
US = CH + H
HALF = CH // 2 + LANES
WIDE = 512
FAR_MID, NEAR_MID = DI // 2, 768
FAR = -1e30
F32 = jnp.float32
BF16 = jnp.bfloat16
VMEM_LIMIT = 56 * 1024 * 1024


def dot_nn(a, b):
    return lax.dot_general(a, b, (((1,), (0,)), ((), ())), preferred_element_type=F32)


def dot_nt(a, b):
    return lax.dot_general(a, b, (((1,), (1,)), ((), ())), preferred_element_type=F32)


def dot_tn(a, b):
    return lax.dot_general(a, b, (((0,), (0,)), ((), ())), preferred_element_type=F32)


def dot_full(a, b):
    return lax.dot_general(
        a, b, (((1,), (0,)), ((), ())), precision=lax.Precision.HIGHEST, preferred_element_type=F32
    )


def two_parts(x):
    high = x.astype(BF16)
    return high, (x - high.astype(F32)).astype(BF16)


def low_lanes():
    return lax.broadcasted_iota(jnp.int32, (Q, LANES), 1) < P_SIZE


def spread(table, first, pair, low):
    a = table[:, first + 2 * pair : first + 2 * pair + 1]
    b = table[:, first + 2 * pair + 1 : first + 2 * pair + 2]
    return jnp.where(low, a, b)


def column(table, index):
    return table[:, index : index + 1]


def lanes_of(index):
    return pl.ds(index * LANES, LANES)


def fold_rows(x):
    return jnp.sum(x.reshape(x.shape[0] // 8, 8, x.shape[1]), axis=0)


STEP, LOGS, TO_END, FROM_START = 0, 32, 64, 96


def front_kernel(
    us_ref, rim_ref, segx_ref, taps_ref, heads_ref, oht_ref, copies_ref,
    act_ref, slope_ref, aux_ref, lt_ref, drow_ref, sout_ref, msg_ref,
    ubuf, state, decay, xbuf,
):
    c = pl.program_id(0)

    @pl.when(c == 0)
    def _():
        ubuf[0:8, :] = rim_ref[...].astype(F32)
        state[...] = jnp.zeros_like(state)
        decay[...] = jnp.ones_like(decay)

    @pl.when(c > 0)
    def _():
        ubuf[0:8, :] = ubuf[Q : Q + 8, :]

    seg_rows = segx_ref[pl.ds(pl.multiple_of(c * Q, Q), Q + 8), :]
    seg = seg_rows[8:]
    masks = [(seg_rows[5 + k : 5 + k + Q] == seg).astype(F32) for k in range(CONV - 1)]
    for j in range(BLOCKS):
        cols = lanes_of(j)
        ubuf[8 : 8 + Q, cols] = us_ref[:, cols].astype(F32)
        filtered = taps_ref[4:5, cols] + taps_ref[3:4, cols] * ubuf[8 : 8 + Q, cols]
        for k in range(CONV - 1):
            filtered += taps_ref[k : k + 1, cols] * (ubuf[5 + k : 5 + k + Q, cols] * masks[k])
        gate = 1.0 / (1.0 + jnp.exp(-filtered))
        active = filtered * gate
        act_ref[:, cols] = active.astype(BF16)
        if j >= PAIRS:
            act_ref[:, lanes_of(j + 2)] = two_parts(active)[1]
        slope_ref[:, cols] = (gate * (1.0 + filtered - active)).astype(BF16)

    raw = dot_nn(us_ref[:, CH:], copies_ref[...]) + heads_ref[0:1, :]
    step = jnp.maximum(raw, 0.0) + jnp.log1p(jnp.exp(-jnp.abs(raw)))
    rows = lax.broadcasted_iota(jnp.int32, (Q, Q), 0)
    lane = lax.broadcasted_iota(jnp.int32, (Q, Q), 1)
    logs = dot_full((rows >= lane).astype(F32), -(step * heads_ref[1:2, :]))
    last = logs[Q - 1 : Q, :]
    joined = (seg_rows[8:9] == seg_rows[7:8]).astype(F32)
    to_end = jnp.exp(last - logs) * (seg == seg[Q - 1 : Q]).astype(F32)
    from_start = jnp.exp(logs) * (joined * (seg == seg[0:1]).astype(F32))
    aux = jnp.where(
        lane < 64, jnp.where(lane < 32, step, logs), jnp.where(lane < 96, to_end, from_start)
    )
    aux_ref[...] = aux
    lt_ref[0] = logs.T[:H, :]
    through = jnp.exp(last) * joined * (seg[Q - 1 : Q] == seg[0:1]).astype(F32)
    before = decay[0:1, :]
    after = before * through
    row16 = lax.broadcasted_iota(jnp.int32, (16, LANES), 0)
    table = jnp.where(row16 == 0, through, jnp.where(row16 == 1, before, after))
    high, rest = two_parts(table)
    drow = dot_nn(high, oht_ref[...]) + dot_nn(rest, oht_ref[...])
    drow_ref[0] = drow[0:8]
    decay[...] = jnp.broadcast_to(after, decay.shape)

    low = low_lanes()
    for j in range(PAIRS):
        scaled = (spread(aux, STEP, j, low) * act_ref[:, lanes_of(j)].astype(F32)).astype(BF16)
        xbuf[:, lanes_of(j)] = (spread(aux, TO_END, j, low) * scaled.astype(F32)).astype(BF16)
    keys = act_ref[:, KEYS].astype(F32).T.astype(BF16)
    held = state[...] * drow[0:1, :] + dot_nn(keys, xbuf[...])
    state[...] = held
    sout_ref[0] = held
    msg_ref[0:N, :] = held
    msg_ref[N : N + 8, :] = jnp.broadcast_to(drow[2:3], (8, DI))


def within_kernel(act_ref, aux_ref, lt_ref, segx_ref, segr_ref, sprev_ref, skip_ref, y_ref):
    c = pl.program_id(0)
    seg = segx_ref[pl.ds(pl.multiple_of(c * Q + 8, 8), Q), :]
    rows = lax.broadcasted_iota(jnp.int32, (Q, Q), 0)
    lane = lax.broadcasted_iota(jnp.int32, (Q, Q), 1)
    bias = jnp.where((rows >= lane) & (seg == segr_ref[0, 0:1, :]), 0.0, FAR)
    reads = act_ref[:, READS]
    reads_both = jnp.concatenate([reads, act_ref[:, READS_REST]], axis=1)
    keys_twice = jnp.concatenate([act_ref[:, KEYS]] * 2, axis=1)
    scores = dot_nt(reads_both, keys_twice) + dot_nt(reads, act_ref[:, KEYS_REST])
    aux = aux_ref[...]
    low = low_lanes()
    has_prev = (c > 0).astype(F32)
    for j in range(PAIRS):
        cols = lanes_of(j)
        weights = [
            (jnp.exp(column(aux, LOGS + h) - lt_ref[0, h : h + 1, :] + bias) * scores).astype(BF16)
            for h in (2 * j, 2 * j + 1)
        ]
        values = act_ref[:, cols].astype(F32)
        scaled = spread(aux, STEP, j, low) * values
        stack = jnp.concatenate(
            [jnp.where(low, scaled, 0.0), jnp.where(low, 0.0, scaled)], axis=0
        ).astype(BF16)
        high, rest = two_parts(sprev_ref[0, :, cols])
        carried = dot_nn(reads_both, jnp.concatenate([high, high], axis=0)) + dot_nn(reads, rest)
        carried *= spread(aux, FROM_START, j, low) * has_prev
        y_ref[:, cols] = (
            dot_nn(jnp.concatenate(weights, axis=1), stack)
            + carried
            + skip_ref[0:1, cols] * values
        )


def gate_kernel(
    offs_ref, yloc_ref, aux_ref, drow_ref, sin_ref, reads_ref, rest_ref, z_ref, gain_ref, resid_ref,
    own_ref, *others
):
    pieces, (y_ref, mine_ref, other_ref, next_ref, gbuf, obuf) = others[:-6], others[-6:]
    i = pl.program_id(0)
    aux = aux_ref[...]
    reads = reads_ref[...]
    reads_both = jnp.concatenate([reads, rest_ref[...]], axis=1)
    low = low_lanes()
    total = jnp.zeros((Q, LANES), F32)
    for j in range(PAIRS):
        cols = lanes_of(j)
        high, rest = two_parts(sin_ref[:, cols])
        carried = dot_nn(reads_both, jnp.concatenate([high, high], axis=0)) + dot_nn(reads, rest)
        y = yloc_ref[:, cols] + carried * (spread(aux, FROM_START, j, low) * drow_ref[0, 1:2, cols])
        y_ref[:, cols] = y
        z = z_ref[:, cols].astype(F32)
        gated = y * (z / (1.0 + jnp.exp(-z)))
        gbuf[:, cols] = gated
        total += gated * gated
    scale = lax.rsqrt(jnp.sum(total, axis=1, keepdims=True) * (1.0 / DI) + EPSILON)
    rows = pl.ds(pl.multiple_of(i * Q, Q), Q)
    for j in range(PAIRS):
        cols = lanes_of(j)
        obuf[rows, cols] = (gbuf[:, cols] * scale * gain_ref[0:1, cols]).astype(BF16)

    @pl.when(i == pl.num_programs(0) - 1)
    def _():
        half, quarter = DI // 2, DI // 4
        core = offs_ref[7]

        def taken(start, width):
            return obuf[:, pl.ds(pl.multiple_of(start, quarter), width)]

        for k, start in enumerate((offs_ref[0], half - offs_ref[0])):
            cols = slice(k * quarter, (k + 1) * quarter)
            mine_ref[:, cols] = taken(start + core * quarter, quarter)
            other_ref[:, cols] = taken(start + (1 - core) * quarter, quarter)
        left = jnp.concatenate(
            [taken(offs_ref[0], half)] + [taken(offs_ref[k + 1], quarter) for k in range(len(pieces))], axis=1
        )
        for j in range(D // 256):
            cols = pl.ds(j * 256, 256)
            right = jnp.concatenate([own_ref[0, :, cols]] + [p[:, cols] for p in pieces], axis=0)
            next_ref[:, cols] = resid_ref[:, cols] + dot_nn(left, right)


def gate_back_kernel(
    offs_ref, grad_ref, y_ref, z_ref, gain_ref, reads_ref, aux_ref, drow_ref, own_ref, *others
):
    pieces, others = others[:-15], others[-15:]
    (dy_ref, rest_ref, dzm_ref, dzo_ref, ggrad_ref, zloc_ref, gmsg_ref, dsuf_ref, low_ref,
     gbuf, grad_state, suffix, xbuf, dout, zbuf) = others
    i = pl.program_id(0)

    @pl.when(i == 0)
    def _():
        low_ref[...] = grad_ref[...].astype(BF16)
        left = low_ref[...]
        for j in range(DI // 512):
            right = own_ref[0, 256 * j : 256 * (j + 1), :]
            cols = pl.ds(pl.multiple_of(offs_ref[0] + 256 * j, 256), 256)
            dout[:, cols] = dot_nt(left, right)
        quarter = DI // 4
        for k, p in enumerate(pieces):
            for j in range(quarter // 256):
                right = p[256 * j : 256 * (j + 1), :]
                cols = pl.ds(pl.multiple_of(offs_ref[k + 1] + 256 * j, 256), 256)
                dout[:, cols] = dot_nt(left, right)
        ggrad_ref[...] = jnp.zeros_like(ggrad_ref)
        grad_state[...] = jnp.zeros_like(grad_state)
        suffix[...] = jnp.ones_like(suffix)

    rows = pl.ds(pl.multiple_of((pl.num_programs(0) - 1 - i) * Q, Q), Q)
    aux = aux_ref[...]
    low = low_lanes()
    total = jnp.zeros((Q, LANES), F32)
    cross = jnp.zeros((Q, LANES), F32)
    for j in range(PAIRS):
        cols = lanes_of(j)
        z = z_ref[:, cols].astype(F32)
        gated = y_ref[:, cols] * (z / (1.0 + jnp.exp(-z)))
        gbuf[:, cols] = gated
        total += gated * gated
        cross += gated * (dout[rows, cols] * gain_ref[0:1, cols])
    scale = lax.rsqrt(jnp.sum(total, axis=1, keepdims=True) * (1.0 / DI) + EPSILON)
    pull = jnp.sum(cross, axis=1, keepdims=True) * (scale * scale * scale * (1.0 / DI))
    scale = jnp.broadcast_to(scale, (Q, LANES))
    pull = jnp.broadcast_to(pull, (Q, LANES))
    for j in range(PAIRS):
        cols = lanes_of(j)
        z = z_ref[:, cols].astype(F32)
        gate = 1.0 / (1.0 + jnp.exp(-z))
        gated = gbuf[:, cols]
        scaled = dout[rows, cols] * scale
        ggrad_ref[:, cols] += fold_rows(scaled * gated)
        d_gated = scaled * gain_ref[0:1, cols] - gated * pull
        dy, rest = two_parts(d_gated * (z * gate))
        dy_ref[:, cols] = dy
        rest_ref[:, cols] = rest
        zbuf[:, cols] = (d_gated * y_ref[:, cols] * (gate * (1.0 + z * (1.0 - gate)))).astype(BF16)
        xbuf[:, cols] = (dy.astype(F32) * spread(aux, FROM_START, j, low)).astype(BF16)
    half, core = DI // 2, offs_ref[7]
    dzm_ref[...] = zbuf[:, pl.ds(pl.multiple_of(core * half, half), half)]
    dzo_ref[...] = zbuf[:, pl.ds(pl.multiple_of((1 - core) * half, half), half)]
    zloc_ref[0] = grad_state[...].astype(BF16)
    dsuf_ref[0] = suffix[...]
    reads = reads_ref[...].astype(F32).T.astype(BF16)
    through = drow_ref[0, 0:1, :]
    grad_state[...] = grad_state[...] * through + dot_nn(reads, xbuf[...])
    suffix[...] = suffix[...] * through
    gmsg_ref[...] = grad_state[...].astype(BF16)


def within_back_kernel(
    act_ref, aux_ref, lt_ref, segx_ref, segr_ref, dy_ref, rest_ref, sprev_ref, drow_ref, sin_ref, zloc_ref,
    dxs_ref, dbc_ref, wbuf, wrest, ibuf, irest, ebuf,
):
    c = pl.program_id(0)
    seg = segx_ref[pl.ds(pl.multiple_of(c * Q + 8, 8), Q), :]
    rows = lax.broadcasted_iota(jnp.int32, (Q, Q), 0)
    lane = lax.broadcasted_iota(jnp.int32, (Q, Q), 1)
    bias = jnp.where((rows <= lane) & (seg == segr_ref[0, 0:1, :]), 0.0, FAR)
    keys, reads = act_ref[:, KEYS], act_ref[:, READS]
    scores = dot_nt(
        jnp.concatenate([keys, keys], axis=1), jnp.concatenate([reads, act_ref[:, READS_REST]], axis=1)
    ) + dot_nt(act_ref[:, KEYS_REST], reads)
    aux = aux_ref[...]
    low = low_lanes()
    has_prev = (c > 0).astype(F32)
    d_scores = jnp.zeros((Q, Q), F32)
    for j in range(PAIRS):
        cols = lanes_of(j)
        fades = [
            jnp.exp(lt_ref[0, h : h + 1, :] - column(aux, LOGS + h) + bias)
            for h in (2 * j, 2 * j + 1)
        ]
        weights = jnp.concatenate([(fade * scores).astype(BF16) for fade in fades], axis=1)
        dy = dy_ref[:, cols]
        dy_wide = dy.astype(F32)
        dy_rest = rest_ref[:, cols]
        stack = jnp.concatenate(
            [jnp.where(low, dy_wide, 0.0), jnp.where(low, 0.0, dy_wide)], axis=0
        ).astype(BF16)
        scaled = (spread(aux, STEP, j, low) * act_ref[:, cols].astype(F32)).astype(BF16).astype(F32)
        both = jnp.concatenate(
            [jnp.where(low, scaled, 0.0), jnp.where(low, 0.0, scaled)], axis=0
        ).astype(BF16)
        d_weights = dot_nt(
            jnp.concatenate([both, both], axis=1), jnp.concatenate([dy, dy_rest], axis=1)
        )
        d_scores += d_weights[:Q] * fades[0] + d_weights[Q:] * fades[1]
        to_end = spread(aux, TO_END, j, low)
        dxs_ref[:, cols] = dot_nn(weights, stack) + to_end * dot_nn(keys, zloc_ref[0, :, cols])
        wbuf[:, cols], wrest[:, cols] = two_parts(
            (dy_wide + dy_rest.astype(F32)) * spread(aux, FROM_START, j, low)
        )
        ebuf[:, cols] = (to_end * scaled).astype(BF16)
        ibuf[:, cols], irest[:, cols] = two_parts(
            drow_ref[0, 1:2, cols] * sin_ref[:, cols] + has_prev * sprev_ref[0, :, cols]
        )
    dbc_ref[:, 0:N] = dot_nn(d_scores.astype(BF16), reads) + dot_nt(ebuf[...], zloc_ref[0])
    high, rest = two_parts(d_scores.T)
    dbc_ref[:, N:] = (
        dot_nn(high, keys)
        + dot_nn(rest, keys)
        + dot_nt(wbuf[...], ibuf[...])
        + dot_nt(wrest[...], ibuf[...])
        + dot_nt(wbuf[...], irest[...])
    )


def last_kernel(
    offs_ref, act_ref, aux_ref, slope_ref, us_ref, rim_ref, segx_ref, taps_ref, heads_ref, skip_ref,
    oh_ref, copies_ref, dy_ref, y_ref, dxs_ref, dbc_ref, sout_ref, drow_ref, sin_ref, zloc_ref, dsuf_ref, zdev_ref,
    dum_ref, duo_ref, tail_ref, rimout_ref, tgrad_ref, hgrad_ref,
    dubuf, dbuf, qhigh, qrest, vhigh, vrest, ebuf, sums, skips,
):
    i = pl.program_id(0)
    count = pl.num_programs(0)
    c = count - 1 - i

    @pl.when(i == 0)
    def _():
        dbuf[Q : Q + 8, :] = jnp.zeros((8, CH), F32)
        tgrad_ref[...] = jnp.zeros_like(tgrad_ref)
        hgrad_ref[...] = jnp.zeros_like(hgrad_ref)
        skips[...] = jnp.zeros_like(skips)

    @pl.when(i > 0)
    def _():
        dbuf[Q : Q + 8, :] = dbuf[0:8, :]

    aux = aux_ref[...]
    low = low_lanes()
    keys = act_ref[:, KEYS]
    for j in range(PAIRS):
        cols = lanes_of(j)
        dy = dy_ref[:, cols].astype(F32)
        values = act_ref[:, cols].astype(F32)
        step = spread(aux, STEP, j, low)
        scaled = (step * values).astype(BF16).astype(F32)
        reach = spread(aux, TO_END, j, low) * dsuf_ref[0, 0:1, cols]
        dxs = dxs_ref[:, cols] + reach * dot_nn(keys, zdev_ref[:, cols])
        ebuf[:, cols] = (reach * scaled).astype(BF16)
        skip = skip_ref[0:1, cols]
        dbuf[0:Q, cols] = (step * dxs + skip * dy) * slope_ref[:, cols].astype(F32)
        qhigh[:, cols], qrest[:, cols] = two_parts(dy * (y_ref[:, cols] - skip * values) - scaled * dxs)
        vhigh[:, cols], vrest[:, cols] = two_parts(values * dxs)
        skips[:, cols] += fold_rows(values * dy)
        arrived = zloc_ref[0, :, cols].astype(F32) + dsuf_ref[0, 0:1, cols] * zdev_ref[:, cols].astype(F32)
        leaving = sout_ref[0, :, cols] + drow_ref[0, 2:3, cols] * sin_ref[:, cols]
        sums[:, cols] = fold_rows(arrived * leaving)
    d_keys = dbc_ref[:, 0:N] + dot_nt(ebuf[...], zdev_ref[...])
    dbuf[0:Q, DI : DI + N] = d_keys * slope_ref[:, DI : DI + N].astype(F32)
    dbuf[0:Q, DI + N :] = dbc_ref[:, N:] * slope_ref[:, DI + N :].astype(F32)

    hot = oh_ref[...]

    def by_head(x):
        high, rest = two_parts(x)
        return dot_nn(high, hot) + dot_nn(rest, hot)

    d_logs = dot_nn(qhigh[...], hot) + dot_nn(qrest[...], hot)
    d_last = jnp.sum(by_head(sums[...]), axis=0, keepdims=True)
    rows = lax.broadcasted_iota(jnp.int32, (Q, Q), 0)
    lane = lax.broadcasted_iota(jnp.int32, (Q, Q), 1)
    d_decay = dot_full((rows <= lane).astype(F32), d_logs) + d_last
    raw = dot_nn(us_ref[:, CH:], copies_ref[...]) + heads_ref[0:1, :]
    step = jnp.maximum(raw, 0.0) + jnp.log1p(jnp.exp(-jnp.abs(raw)))
    d_step = dot_nn(vhigh[...], hot) + dot_nn(vrest[...], hot) - heads_ref[1:2, :] * d_decay
    d_raw = d_step / (1.0 + jnp.exp(-raw))
    d_raw = jnp.where(lane < H, d_raw, 0.0).astype(BF16)
    dum_ref[:, CH // 2 :] = d_raw
    duo_ref[:, CH // 2 :] = d_raw
    hgrad_ref[0:8, :] += fold_rows(d_raw)
    hgrad_ref[8:16, :] += fold_rows(-(step * d_decay))

    @pl.when(i == count - 1)
    def _():
        hgrad_ref[16:24, :] = by_head(skips[...])

    seg_rows = segx_ref[pl.ds(pl.multiple_of(c * Q + 8, 8), Q + 8), :]
    seg = seg_rows[:Q]
    masks = [(seg_rows[m : m + Q] == seg).astype(F32) for m in range(1, CONV)]
    for j in range(BLOCKS):
        cols = lanes_of(j)
        d_filtered = dbuf[0:Q, cols]
        u = us_ref[:, cols].astype(F32)
        du = taps_ref[3:4, cols] * d_filtered
        tgrad_ref[24:32, cols] += fold_rows(u * d_filtered)
        tgrad_ref[32:40, cols] += fold_rows(d_filtered)
        for m in range(1, CONV):
            later = dbuf[m : m + Q, cols] * masks[m - 1]
            du += taps_ref[3 - m : 4 - m, cols] * later
            tgrad_ref[8 * (3 - m) : 8 * (4 - m), cols] += fold_rows(u * later)
        dubuf[:, cols] = du.astype(BF16)

        @pl.when(i == 0)
        def _():
            tail_ref[:, cols] = du[Q - 8 :]

    half, core = CH // 2, offs_ref[7]
    dum_ref[:, :half] = dubuf[:, pl.ds(pl.multiple_of(core * half, LANES), half)]
    duo_ref[:, :half] = dubuf[:, pl.ds(pl.multiple_of((1 - core) * half, LANES), half)]

    @pl.when(i == count - 1)
    def _():
        near = segx_ref[0:16, :]
        rim_masks = [(near[m : m + 8] == near[0:8]).astype(F32) for m in range(1, CONV)]
        for j in range(BLOCKS):
            cols = lanes_of(j)
            edge = jnp.concatenate([jnp.zeros((8, LANES), F32), dbuf[0:8, cols]], axis=0)
            u = rim_ref[:, cols].astype(F32)
            out = jnp.zeros((8, LANES), F32)
            for m in range(1, CONV):
                later = edge[m : m + 8] * rim_masks[m - 1]
                out += taps_ref[3 - m : 4 - m, cols] * later
                tgrad_ref[8 * (3 - m) : 8 * (4 - m), cols] += u * later
            rimout_ref[:, cols] = out.astype(BF16)


def expand_first_kernel(offs_ref, resid_ref, gain_ref, own_ref, *others):
    pieces, (out_ref, normed_ref, left) = others[:-3], others[-3:]
    half = D // 2

    @pl.when(pl.program_id(0) == 0)
    def _():
        x = resid_ref[...]
        scale = lax.rsqrt(jnp.mean(x * x, axis=1, keepdims=True) + EPSILON)
        left[...] = (x * scale * gain_ref[...]).astype(BF16)
        own = left[:, pl.ds(pl.multiple_of(offs_ref[0], half), half)]
        normed_ref[:, half:] = left[:, pl.ds(pl.multiple_of(half - offs_ref[0], half), half)]
        normed_ref[:, :half] = own

    out_ref[...] = expand_block(offs_ref, normed_ref, own_ref, pieces).astype(BF16)


def expand_block(offs_ref, normed_ref, own_ref, pieces):
    half = D // 2
    parts = [normed_ref[:, :half]]
    for k, p in enumerate(pieces):
        at = half + lax.rem(offs_ref[k + 1], half)
        parts.append(normed_ref[:, pl.ds(pl.multiple_of(at, LANES), p.shape[1])])
    right = jnp.concatenate([own_ref[0]] + [p[...] for p in pieces], axis=1)
    return dot_nt(jnp.concatenate(parts, axis=1), right)


def expand_rest_kernel(offs_ref, normed_ref, own_ref, *others):
    pieces, out_ref = others[:-1], others[-1]
    out_ref[...] = expand_block(offs_ref, normed_ref, own_ref, pieces).astype(BF16)


def input_back_kernel(
    count, layer, offs_ref, dzm_ref, dzo_ref, dum_ref, duo_ref, gain_ref, resid_ref, grad_ref, own_ref, *others
):
    near, far = others[:count], others[count : 2 * count]
    (next_ref, ngrad_ref, own, *bufs), (dn, sems) = others[2 * count : -2], others[-2:]
    near_bufs, far_bufs = bufs[:count], bufs[count:]
    moves = [(own_ref.at[layer], own)] + list(zip(near, near_bufs))
    moves += list(zip(far, far_bufs))
    copies = [pltpu.make_async_copy(src, dst, sems.at[k]) for k, (src, dst) in enumerate(moves)]
    for copy in copies:
        copy.start()
    copies[0].wait()
    core, zs, us = offs_ref[7], DI // 2, CH // 2
    parts = [
        (dzm_ref[...], 0, core * zs), (dzo_ref[...], 0, (1 - core) * zs),
        (dum_ref[:, :us], DI, core * us), (duo_ref[:, :us], DI, (1 - core) * us), (dum_ref[:, us : us + H], DI + CH, 0),
    ]

    def down(part, buf, base):
        left, start, at = part
        if not isinstance(at, int):
            at = pl.multiple_of(at, LANES)
        return dot_nn(left, buf[pl.ds(start - base + at, left.shape[1]), base_cols])

    for j in range(D // 2 // 256):
        base_cols = slice(j * 256, (j + 1) * 256)
        cols = pl.ds(pl.multiple_of(offs_ref[0] + j * 256, 256), 256)
        dn[:, cols] = sum(down(part, own, 0) for part in parts)
    base_cols = slice(None)
    for k in range(count):
        copies[1 + k].wait()
        copies[1 + count + k].wait()
        cols = pl.ds(pl.multiple_of(offs_ref[k + 1], LANES), near_bufs[k].shape[1])
        dn[:, cols] = sum(down(part, far_bufs[k], 0) for part in parts[:2]) + sum(
            down(part, near_bufs[k], DI) for part in parts[2:]
        )
    ngrad = jnp.zeros((8, D), F32)
    for i in range(dzm_ref.shape[0] // Q):
        rows = slice(i * Q, (i + 1) * Q)
        x = resid_ref[rows, :]
        scale = lax.rsqrt(jnp.mean(x * x, axis=1, keepdims=True) + EPSILON)
        unit = x * scale
        down = dn[rows, :]
        ngrad += fold_rows(down * unit)
        pulled = down * gain_ref[...]
        mean = jnp.mean(pulled * unit, axis=1, keepdims=True)
        next_ref[rows, :] = grad_ref[rows, :] + scale * (pulled - unit * mean)
    ngrad_ref[...] = ngrad


def rows_at(which, size, base=0):
    return pl.ds(pl.multiple_of(base + which * size, 16), size)


def weight_grads(i, count, offs_ref, left, right, away_left, away_right, own_ref, away_ref, near_ref, far_ref):
    size, width = own_ref.shape
    first = near_ref.shape[0] // size
    mine = dot_tn(left, right).astype(BF16)
    away = dot_tn(away_left, away_right).astype(BF16)
    own_ref[...] = mine
    away_ref[...] = away

    @pl.when(i < first)
    def _():
        near_ref[rows_at(i, size), :] = away

    start = first + (1 - offs_ref[6]) * (far_ref.shape[0] // size)

    @pl.when((i >= start) & (i < start + far_ref.shape[0] // size))
    def _():
        far_ref[rows_at(i - start, size), :width] = mine
        far_ref[rows_at(i - start, size), width:] = away


def both_of(pair, lanes):
    return jnp.concatenate([ref[:, lanes] for ref in pair], axis=0)


def far_grads_kernel(offs_ref, dzm, dzr, nm, nr, om, orr, lm, lr, *outs):
    i = pl.program_id(0)
    half, size = D // 2, 256

    @pl.when(i < 4)
    def _():
        left = both_of((dzm, dzr), pl.ds(pl.multiple_of(i * size, size), size))
        weight_grads(
            i, 8, offs_ref, left, both_of((nm, nr), slice(0, half)), left, both_of((nm, nr), slice(half, D)), *outs
        )

    @pl.when(i >= 4)
    def _():
        at = lax.rem(i, 2) * size
        right = both_of((lm, lr), pl.ds(pl.multiple_of((i - 4) // 2 * half, half), half))
        left = both_of((om, orr), pl.ds(pl.multiple_of(at, size), size))
        away = both_of((om, orr), pl.ds(pl.multiple_of(half + at, size), size))
        weight_grads(i, 8, offs_ref, left, right, away, right, *outs)


def near_grads_kernel(offs_ref, dum, dur, nm, nr, *outs):
    i = pl.program_id(0)
    half, size = D // 2, 256
    left = both_of((dum, dur), pl.ds(pl.multiple_of(i * size, size), size))
    weight_grads(
        i, 5, offs_ref, left, both_of((nm, nr), slice(0, half)), left, both_of((nm, nr), slice(half, D)), *outs
    )


def rows_at(which, size, base=0):
    return pl.ds(pl.multiple_of(base + which * size, LANES), size)


def cross_kernel(offs_ref, own_ref, away_ref, near_ref, far_ref, keep_ref, to_rep_ref, to_fsdp_ref):
    mid, width = near_ref.shape
    first, second, rep = to_rep_ref.shape[0], to_fsdp_ref.shape[0], offs_ref[6]
    for ref, which in ((keep_ref, rep), (to_rep_ref, 1 - rep)):
        rows = rows_at(which, first)
        total = own_ref[rows, :].astype(F32) + near_ref[rows, :].astype(F32)
        ref[:first, :] = total.astype(ref.dtype)
    rows = rows_at(rep, second, mid)
    keep_ref[first:, :] = own_ref[rows, :].astype(F32) + far_ref[:, :width].astype(F32)
    to_fsdp_ref[...] = (away_ref[rows, :].astype(F32) + far_ref[:, width:].astype(F32)).astype(BF16)


def meet_kernel(keep_ref, a_ref, b_ref, out_ref):
    size = a_ref.shape[0]
    out_ref[:size, :] = (keep_ref[:size, :] + a_ref[...].astype(F32)).astype(BF16)
    out_ref[size:, :] = (keep_ref[size:, :] + b_ref[...].astype(F32)).astype(BF16)


def take_kernel(lanes, offs_ref, src_ref, out_ref):
    rows, width = out_ref.shape
    core = offs_ref[7]
    if lanes:
        out_ref[...] = src_ref[0, :, pl.ds(pl.multiple_of(core * width, width), width)]
    else:
        out_ref[...] = src_ref[0, rows_at(core, rows), :]


def reduce_kernel(parts_ref, out_ref):
    count, rows = parts_ref.shape[0], parts_ref.shape[1]
    total = parts_ref[0].astype(F32)
    for k in range(1, count):
        total += parts_ref[k].astype(F32)
    total = total.astype(BF16)
    for k in range(count):
        out_ref[k * rows : (k + 1) * rows, :] = total


def final_kernel(layer, count, offs_ref, *others):
    far, near = others[:count], others[count : 2 * count]
    expand_ref, reduce_ref, zbuf, ubuf, sbuf, rbuf, sems = others[-7:]
    core, rep, zs, us, rs = offs_ref[7], offs_ref[6], DI // 2, CH // 2, DI // 4
    copies = []

    def put(src, ref, start, size):
        copy = pltpu.make_async_copy(src, ref.at[layer, pl.ds(start, size)], sems.at[len(copies)])
        copy.start()
        copies.append(copy)

    for k in range(2):
        which = core if k == 0 else 1 - core
        for h in range(2):
            at = rep if h == 0 else 1 - rep
            for buf, part, mid in ((zbuf, far[2 * k + h], FAR_MID), (ubuf, near[2 * k + h], NEAR_MID)):
                size = mid // 2
                buf[k, rows_at(at, size), :] = part[:size, :].astype(F32)
                buf[k, rows_at(at, part.shape[0] - size, mid), :] = part[size:, :].astype(F32)
        for q in range(2):
            rbuf[k, :, 512 * q : 512 * (q + 1)] = zbuf[k, zs + rs * q : zs + rs * (q + 1), :]
        put(rbuf.at[k], reduce_ref, pl.multiple_of(which * rs, LANES), rs)
        put(zbuf.at[k, pl.ds(0, zs)], expand_ref, pl.multiple_of(which * zs, LANES), zs)
        put(ubuf.at[k, pl.ds(0, us)], expand_ref, pl.multiple_of(DI + which * us, LANES), us)
    sbuf[...] = ubuf[0, us : us + H, :]
    put(sbuf, expand_ref, DI + CH, H)
    for copy in copies:
        copy.wait()


def whole(shape):
    return pl.BlockSpec(shape, lambda i: (0,) * len(shape))


def by_rows(shape, count=None):
    if count is None:
        return pl.BlockSpec(shape, lambda i: (i,) + (0,) * (len(shape) - 1))
    return pl.BlockSpec(shape, lambda i: (count - 1 - i,) + (0,) * (len(shape) - 1))


def struct(shape, dtype):
    return jax.ShapeDtypeStruct(shape, dtype)


SCALARS = pl.BlockSpec(memory_space=pltpu.SMEM)
ANYWHERE = pl.BlockSpec(memory_space=pl.ANY)


COST = {
    "expand_first": 8, "ssd_front": 13, "expand_rest": 6, "ssd_within": 11, "ssd_gate": 13, "gate_back": 15,
    "within_back": 17, "ssd_last": 24, "input_back": 16, "far_grads": 12, "near_grads": 6, "take": 1, "cross": 4, "meet": 3, "reduce_parts": 2,
    "final_grads": 8,
}


def call(kernel, grid, in_specs, out_specs, out_shape, scratch, name, deps=(), aliases=None):
    n, m = len(in_specs), len(deps)

    def body(*refs):
        kernel(*refs[:n], *refs[n + m :])

    run = pl.pallas_call(
        body,
        grid=(grid,),
        in_specs=list(in_specs) + [ANYWHERE] * m,
        out_specs=out_specs,
        out_shape=out_shape,
        scratch_shapes=scratch,
        input_output_aliases=aliases or {},
        compiler_params=pltpu.CompilerParams(
            dimension_semantics=("arbitrary",), vmem_limit_bytes=VMEM_LIMIT
        ),
        cost_estimate=pl.CostEstimate(
            flops=int(COST[name] * 1.1e9), bytes_accessed=1000, transcendentals=0
        ),
        name=name,
    )
    return lambda *args: run(*args, *deps)


def expand_first(offs, resid, gain, own, pieces, layer):
    T = resid.shape[0]
    first = DI // WIDE
    return call(
        expand_first_kernel, -(-US // WIDE),
        [SCALARS, whole((T, D)), whole((1, D)),
         pl.BlockSpec((1, WIDE, D // 2), lambda i: (layer, first + i, 0))]
        + [pl.BlockSpec((WIDE, p.shape[1]), lambda i: (i, 0)) for p in pieces],
        [pl.BlockSpec((T, WIDE), lambda i: (0, i)), whole((T, D))],
        [struct((T, US), BF16), struct((T, D), BF16)],
        [pltpu.VMEM((T, D), BF16)],
        "expand_first",
    )(offs, resid, gain, own, *pieces)


def expand_rest(offs, normed, own, pieces, layer, deps=()):
    T = normed.shape[0]
    return call(
        expand_rest_kernel, DI // WIDE,
        [SCALARS, whole((T, D)), pl.BlockSpec((1, WIDE, D // 2), lambda i: (layer, i, 0))]
        + [pl.BlockSpec((WIDE, p.shape[1]), lambda i: (i, 0)) for p in pieces],
        pl.BlockSpec((T, WIDE), lambda i: (0, i)),
        struct((T, DI), BF16), [],
        "expand_rest", deps,
    )(offs, normed, own, *pieces)


def input_back(offs, dzm, dzo, dum, duo, gain, resid, grad, own, near, far, layer, deps=()):
    T = dzm.shape[0]
    count = len(near)
    return call(
        functools.partial(input_back_kernel, count, layer), 1,
        [SCALARS] + [whole(a.shape) for a in (dzm, dzo, dum, duo)]
        + [whole((1, D)), whole((T, D)), whole((T, D)), ANYWHERE] + [ANYWHERE] * (2 * count),
        [whole((T, D)), whole((8, D))],
        [struct((T, D), F32), struct((8, D), F32)],
        [pltpu.VMEM((E, D // 2), BF16)] + [pltpu.VMEM((US, p.shape[1]), BF16) for p in near]
        + [pltpu.VMEM((DI, p.shape[1]), BF16) for p in far]
        + [pltpu.VMEM((T, D), F32), pltpu.SemaphoreType.DMA((1 + 2 * count,))],
        "input_back", deps,
    )(offs, dzm, dzo, dum, duo, gain, resid, grad, own, *near, *far)


def final_grads(offs, far, near, layer, held, deps=()):
    n = 1 + len(far) + len(near)
    return call(
        functools.partial(final_kernel, layer, len(far)), 1,
        [SCALARS] + [whole(p.shape) for p in (*far, *near)] + [ANYWHERE] * len(held),
        [ANYWHERE, ANYWHERE],
        [struct((LAYERS, E, D // 2), F32), struct((LAYERS, DI // 2, D), F32)],
        [pltpu.VMEM((2, DI, D // 2), F32), pltpu.VMEM((2, HALF, D // 2), F32),
         pltpu.VMEM((H, D // 2), F32), pltpu.VMEM((2, DI // 4, D), F32), pltpu.SemaphoreType.DMA((7,))],
        "final_grads", deps,
        aliases={n + k: k for k in range(len(held))},
    )(offs, *far, *near, *held)


class Sum:
    def __init__(self, offs, name, kernel, args, mid, deps=()):
        rows, width, size = (DI if name == "far_grads" else HALF), D // 2, 256
        block = by_rows((size, width))
        shapes = [(rows, width), (rows, width), (mid, width), ((rows - mid) // 2, 2 * width)]
        self.offs = offs
        self.own, self.away, near, far = call(
            kernel, rows // size, [SCALARS] + [whole(a.shape) for a in args],
            [block, block] + [whole(shape) for shape in shapes[2:]], [struct(shape, BF16) for shape in shapes],
            [], name, deps,
        )(offs, *args)
        self.near, self.far = swap(near, "fsdp"), swap(far, "rep")

    def cross(self, deps=()):
        mid, width = self.near.shape
        first, second = mid // 2, self.far.shape[0]
        shapes = [(first + second, width), (first, width), (second, width)]
        args = (self.own, self.away, self.near, self.far)
        self.keep, to_rep, to_fsdp = call(
            cross_kernel, 1, [SCALARS] + [whole(a.shape) for a in args], [whole(shape) for shape in shapes],
            [struct(shapes[0], F32)] + [struct(shape, BF16) for shape in shapes[1:]], [], "cross", deps,
        )(self.offs, *args)
        self.a, self.b = swap(to_rep, "rep"), swap(to_fsdp, "fsdp")
        return (to_rep,)

    def meet(self, deps=()):
        args = (self.keep, self.a, self.b)
        total = call(
            meet_kernel, 1, [whole(a.shape) for a in args], whole(self.keep.shape), struct(self.keep.shape, BF16),
            [], "meet", deps,
        )(*args)
        self.parts = lax.all_to_all(total, "zz", 0, 0, tiled=True)
        return (total,)

    def reduce(self, deps=()):
        rows, width = self.parts.shape
        count = lax.axis_size("zz")
        copies = reduce_parts(self.parts.reshape(count, rows // count, width), deps)
        self.mine = lax.all_to_all(copies, "zz", 0, 0, tiled=True)
        return (copies,)

    def spread(self, other=None):
        parts = [self.mine, swap(self.mine, "rep") if other is None else other]
        return parts + [swap(p, "core") for p in parts]


def reduce_parts(parts, deps):
    count, rows, width = parts.shape
    return call(
        reduce_kernel, 1, [whole(parts.shape)], whole((count * rows, width)),
        struct((count * rows, width), BF16), [], "reduce_parts", deps,
    )(parts)


def ssd_front(us, rim, segx, taps, heads, oht, copies, deps=()):
    T = us.shape[0]
    nc = T // Q
    return call(
        front_kernel, nc,
        [by_rows((Q, US)), whole((8, CH)), whole(segx.shape), whole(taps.shape),
         whole(heads.shape), whole(oht.shape), whole(copies.shape)],
        [by_rows((Q, ACT)), by_rows((Q, CH)), by_rows((Q, LANES)), by_rows((1, H, Q)),
         by_rows((1, 8, DI)), by_rows((1, N, DI)), whole((N + 8, DI))],
        [struct((T, ACT), BF16), struct((T, CH), BF16), struct((T, LANES), F32), struct((nc, H, Q), F32),
         struct((nc, 8, DI), F32), struct((nc, N, DI), F32), struct((N + 8, DI), F32)],
        [pltpu.VMEM((Q + 8, CH), F32), pltpu.VMEM((N, DI), F32), pltpu.VMEM((8, LANES), F32),
         pltpu.VMEM((Q, DI), BF16)],
        "ssd_front", deps,
    )(us, rim, segx, taps, heads, oht, copies)


def previous(shape):
    return pl.BlockSpec(shape, lambda i: (jnp.maximum(i - 1, 0), 0, 0))


def ssd_within(act, aux, lt, segx, segr, sout, skip, deps=()):
    T = act.shape[0]
    nc = T // Q
    return call(
        within_kernel, nc,
        [by_rows((Q, ACT)), by_rows((Q, LANES)), by_rows((1, H, Q)), whole(segx.shape),
         by_rows((1, 8, LANES)), previous((1, N, DI)), whole(skip.shape)],
        by_rows((Q, DI)), struct((T, DI), F32), [],
        "ssd_within", deps,
    )(act, aux, lt, segx, segr, sout, skip)


def ssd_gate(offs, yloc, aux, drow, s_in, act, z, gain, resid, own, pieces, layer):
    T = yloc.shape[0]
    nc = T // Q
    reads = pl.BlockSpec((Q, N), lambda i: (i, READS.start // N))
    rest = pl.BlockSpec((Q, N), lambda i: (i, READS_REST.start // N))
    return call(
        gate_kernel, nc,
        [SCALARS, by_rows((Q, DI)), by_rows((Q, LANES)), by_rows((1, 8, DI)), whole((N, DI)), reads,
         rest, by_rows((Q, DI)), whole(gain.shape), whole((T, D)),
         pl.BlockSpec((1, DI // 2, D), lambda i: (layer, 0, 0))] + [whole(p.shape) for p in pieces],
        [by_rows((Q, DI)), whole((T, DI // 2)), whole((T, DI // 2)), whole((T, D))],
        [struct((T, DI), F32), struct((T, DI // 2), BF16), struct((T, DI // 2), BF16), struct((T, D), F32)],
        [pltpu.VMEM((Q, DI), F32), pltpu.VMEM((T, DI), BF16)],
        "ssd_gate",
    )(offs, yloc, aux, drow, s_in, act, act, z, gain, resid, own, *pieces)


def gate_back(offs, grad, y, z, gain, act, aux, drow, own, pieces, layer, deps=()):
    T = y.shape[0]
    nc = T // Q
    reads = pl.BlockSpec((Q, N), lambda i: (nc - 1 - i, READS.start // N))
    return call(
        gate_back_kernel, nc,
        [SCALARS, whole((T, D)), by_rows((Q, DI), nc), by_rows((Q, DI), nc), whole(gain.shape), reads,
         by_rows((Q, LANES), nc), by_rows((1, 8, DI), nc),
         pl.BlockSpec((1, DI // 2, D), lambda i: (layer, 0, 0))] + [whole(p.shape) for p in pieces],
        [by_rows((Q, DI), nc)] * 2 + [by_rows((Q, DI // 2), nc)] * 2 + [whole((8, DI)), by_rows((1, N, DI), nc),
         whole((N, DI)), by_rows((1, 8, DI), nc), whole((T, D))],
        [struct((T, DI), BF16)] * 2 + [struct((T, DI // 2), BF16)] * 2
        + [struct((8, DI), F32), struct((nc, N, DI), BF16),
         struct((N, DI), BF16), struct((nc, 8, DI), F32), struct((T, D), BF16)],
        [pltpu.VMEM((Q, DI), F32), pltpu.VMEM((N, DI), F32), pltpu.VMEM((8, DI), F32),
         pltpu.VMEM((Q, DI), BF16), pltpu.VMEM((T, DI), F32), pltpu.VMEM((Q, DI), BF16)],
        "gate_back", deps,
    )(offs, grad, y, z, gain, act, aux, drow, own, *pieces)


def within_back(act, aux, lt, segx, segr, dy, rest, sout, drow, s_in, zloc, deps=()):
    T = act.shape[0]
    nc = T // Q
    return call(
        within_back_kernel, nc,
        [by_rows((Q, ACT)), by_rows((Q, LANES)), by_rows((1, H, Q)), whole(segx.shape),
         by_rows((1, 8, LANES)), by_rows((Q, DI)), by_rows((Q, DI)), previous((1, N, DI)), by_rows((1, 8, DI)),
         whole((N, DI)), by_rows((1, N, DI))],
        [by_rows((Q, DI)), by_rows((Q, 2 * N))],
        [struct((T, DI), F32), struct((T, 2 * N), F32)],
        [pltpu.VMEM((Q, DI), BF16)] * 5,
        "within_back", deps,
    )(act, aux, lt, segx, segr, dy, rest, sout, drow, s_in, zloc)


def ssd_last(offs, act, aux, slope, us, rim, segx, taps, heads, skip, oh, copies, dy, y, dxs, dbc, sout, drow, s_in,
             zloc, dsuf, zdev, deps=()):
    T = act.shape[0]
    nc = T // Q
    return call(
        last_kernel, nc,
        [SCALARS, by_rows((Q, ACT), nc), by_rows((Q, LANES), nc), by_rows((Q, CH), nc), by_rows((Q, US), nc),
         whole((8, CH)), whole(segx.shape), whole(taps.shape),
         whole(heads.shape), whole(skip.shape), whole(oh.shape), whole(copies.shape), by_rows((Q, DI), nc),
         by_rows((Q, DI), nc), by_rows((Q, DI), nc), by_rows((Q, 2 * N), nc), by_rows((1, N, DI), nc),
         by_rows((1, 8, DI), nc), whole((N, DI)), by_rows((1, N, DI), nc), by_rows((1, 8, DI), nc),
         whole((N, DI))],
        [by_rows((Q, HALF), nc)] * 2 + [whole((8, CH)), whole((8, CH)), whole((40, CH)),
         whole((24, LANES))],
        [struct((T, HALF), BF16)] * 2 + [struct((8, CH), F32), struct((8, CH), BF16),
         struct((40, CH), F32), struct((24, LANES), F32)],
        [pltpu.VMEM((Q, CH), BF16), pltpu.VMEM((Q + 8, CH), F32)] + [pltpu.VMEM((Q, DI), BF16)] * 5
        + [pltpu.VMEM((8, DI), F32), pltpu.VMEM((8, DI), F32)],
        "ssd_last", deps,
    )(offs, act, aux, slope, us, rim, segx, taps, heads, skip, oh, copies, dy, y, dxs, dbc, sout, drow, s_in,
      zloc, dsuf, zdev)


def swap(value, axis):
    return lax.ppermute(value, axis, [(0, 1), (1, 0)])


def flip(value, axis, bit):
    size = lax.axis_size(axis)
    return lax.ppermute(value, axis, [(i, i ^ bit) for i in range(size)])


def ordered(index, mine, other, axis):
    return jnp.where(
        index == 0, jnp.concatenate([mine, other], axis), jnp.concatenate([other, mine], axis)
    )


CTX = ("zz", "core")


def routes():
    n = lax.axis_size("zz") * lax.axis_size("core")
    half = n // 2
    first = [(i, i // 2 + (half if i % 2 else 0)) for i in range(n)]
    second = [(i, i // 2 + (0 if i % 2 else half)) for i in range(n)]
    return half, first, second


def gather_tokens(x):
    half, first, second = routes()
    me = lax.axis_index(CTX)
    even = me % 2 == 0
    a = lax.ppermute(jnp.where(even, x[0], x[1]), CTX, first)
    b = lax.ppermute(jnp.where(even, x[1], x[0]), CTX, second)
    early = me < half
    return jnp.concatenate([jnp.where(early, a, b), jnp.where(early, b, a)], axis=0)


def scatter_tokens(x):
    half, first, second = routes()
    me = lax.axis_index(CTX)
    early = me < half
    rows = x.shape[0] // 2
    x0, x1 = x[:rows], x[rows:]
    a = lax.ppermute(jnp.where(early, x0, x1), CTX, [(d, s) for s, d in first])
    b = lax.ppermute(jnp.where(early, x1, x0), CTX, [(d, s) for s, d in second])
    even = me % 2 == 0
    return jnp.stack([jnp.where(even, a, b), jnp.where(even, b, a)])


def next_piece(value, backward=False):
    n = lax.axis_size("zz") * lax.axis_size("core")
    half = n // 2
    pairs = [(i, i + 1) for i in range(n - 1) if i + 1 != half]
    if backward:
        pairs = [(d, s) for s, d in pairs]
    return lax.ppermute(value, CTX, pairs)


def after(value, earlier):
    value, _ = lax.optimization_barrier((value, earlier))
    return value


def fetch(part):
    got = swap(part, "fsdp")
    return got, swap(got, "core")


def carry_forward(core, msg):
    other = swap(msg, "core")

    s_mine, d_mine = msg[:N], msg[N : N + 1]
    s_other, d_other = other[:N], other[N : N + 1]
    lead = core == 0
    s_first, d_first = jnp.where(lead, s_mine, s_other), jnp.where(lead, d_mine, d_other)
    s_second, d_second = jnp.where(lead, s_other, s_mine), jnp.where(lead, d_other, d_mine)
    total = d_second * s_first + s_second
    through = d_first * d_second
    chips = lax.axis_size("zz") // 2
    total = halves(total, core, 0)[0]
    prefix = jnp.zeros_like(total)
    for hop in range(1, chips):
        sent = total if hop == 1 else through * prefix + total
        pairs = [(hop - 1, hop), (chips + hop - 1, chips + hop)]
        prefix = prefix + lax.ppermute(sent, "zz", pairs)
    prefix = ordered(core, prefix, swap(prefix, "core"), 0)
    incoming = jnp.where(lead, prefix, d_first * prefix + s_first)
    return incoming, (d_first, d_second)


def carry_backward(core, msg, decays):
    other = swap(msg, "core")
    d_first, d_second = decays
    lead = core == 0
    g_first = jnp.where(lead, msg, other).astype(F32)
    g_second = jnp.where(lead, other, msg).astype(F32)
    total = g_first + d_first * g_second
    through = d_first * d_second
    chips = lax.axis_size("zz") // 2
    suffix = jnp.zeros_like(total)
    for hop in range(1, chips):
        sent = total if hop == 1 else through * suffix + total
        pairs = [(chips - hop, chips - hop - 1), (2 * chips - hop, 2 * chips - hop - 1)]
        suffix = suffix + lax.ppermute(sent.astype(BF16), "zz", pairs).astype(F32)
    arriving = jnp.where(lead, g_second + d_second * suffix, suffix)
    return arriving.astype(BF16)


def rms_parts(values):
    return lax.rsqrt(jnp.mean(values * values, axis=-1, keepdims=True) + EPSILON)


def halves(array, index, axis):
    size = array.shape[axis] // 2
    mine = lax.dynamic_slice_in_dim(array, index * size, size, axis)
    other = lax.dynamic_slice_in_dim(array, (1 - index) * size, size, axis)
    return mine, other


def levels():
    out = [("rep", 1)]
    bit = 1
    while bit < lax.axis_size("zz"):
        out.append(("zz", bit))
        bit *= 2
    return out


def following(value, *others):
    for other in others:
        mark = other[0, 0]
        value = jnp.where(mark != mark, jnp.zeros_like(value), value)
    return value


def local(
    tokens,
    segments,
    expand_weight,
    reduce_weight,
    filter_taps,
    filter_offset,
    step_bias,
    decay_rate,
    skip_gain,
    norm_gain,
    gate_gain,
    cotangent,
):
    rows = tokens.shape[1]
    T = 2 * rows
    rep = lax.axis_index("rep")
    fsdp = lax.axis_index("fsdp")
    core = lax.axis_index("core")
    me = lax.axis_index(CTX)
    n = lax.axis_size("zz") * lax.axis_size("core")
    half = n // 2

    def pad(x, width):
        return jnp.pad(x, ((0, 0), (0, 0), (0, width - x.shape[-1])))

    heads_packed = jnp.concatenate([step_bias, decay_rate, skip_gain], axis=-1)
    own = jnp.concatenate(
        [filter_taps, filter_offset[:, None], pad(norm_gain[:, None], CH // 2),
         pad(gate_gain[:, None], CH // 2), pad(heads_packed[:, None], CH // 2)], axis=1
    )
    other = swap(own, "fsdp")
    lead = fsdp == 0
    low_half = jnp.where(lead, own, other).astype(F32)
    high_half = jnp.where(lead, other, own).astype(F32)

    def joined(row, start, size):
        return jnp.concatenate(
            [low_half[:, row, start : start + size], high_half[:, row, start : start + size]], axis=-1
        )

    taps_all = jnp.concatenate([low_half[:, :5], high_half[:, :5]], axis=-1)
    taps_all = jnp.pad(taps_all, ((0, 0), (0, 3), (0, 0)))
    norm_all, gate_all = joined(5, 0, D // 2), joined(6, 0, DI // 2)
    bias_all, rate_all, skip_all = joined(7, 0, H // 2), joined(7, H // 2, H // 2), joined(7, H, H // 2)
    heads_all = jnp.pad(
        jnp.stack([jnp.tile(bias_all, (1, 4)), jnp.tile(rate_all, (1, 4))], axis=1), ((0, 0), (0, 6), (0, 0))
    )
    skip_rows = jnp.repeat(skip_all, P_SIZE, axis=-1)

    hot = (
        lax.broadcasted_iota(jnp.int32, (DI, LANES), 0) // P_SIZE
        == lax.broadcasted_iota(jnp.int32, (DI, LANES), 1)
    ).astype(BF16)
    hot_t = (
        lax.broadcasted_iota(jnp.int32, (LANES, DI), 1) // P_SIZE
        == lax.broadcasted_iota(jnp.int32, (LANES, DI), 0)
    ).astype(BF16)

    copies = (
        lax.broadcasted_iota(jnp.int32, (H, LANES), 0) == lax.broadcasted_iota(jnp.int32, (H, LANES), 1) % H
    ).astype(BF16)

    seq = (me >= half).astype(jnp.int32)
    padded = jnp.pad(segments, ((0, 0), (8, 8)), constant_values=-1)
    seg_line = lax.dynamic_slice(padded, (seq, (me % half) * T), (1, T + 16))[0].astype(F32)
    segx = jnp.broadcast_to(seg_line[:, None], (T + 16, LANES))
    segr = jnp.broadcast_to(seg_line[8 : 8 + T].reshape(T // Q, 1, Q), (T // Q, 8, Q))

    expand_t = jnp.swapaxes(expand_weight, 1, 2)
    quarter = D // 4

    def offsets(size):
        start, away = fsdp * size, (1 - fsdp) * size
        zero = jnp.zeros_like(core)
        return jnp.stack(
            [start, away + core * (size // 2), away + (1 - core) * (size // 2), zero, zero, zero, rep, core]
        ).astype(jnp.int32)

    offs, wide_offs = offsets(D // 2), offsets(DI // 2)

    def take_lanes(layer, start, rows, deps):
        size = 512
        return call(
            functools.partial(take_kernel, True), -(-rows // size),
            [SCALARS, pl.BlockSpec((1, size, D // 2), lambda i: (layer, start // size + i, 0))],
            by_rows((size, quarter)), struct((rows, quarter), BF16), [], "take", deps,
        )(offs, expand_t)

    def take_rows(layer, deps):
        return call(
            functools.partial(take_kernel, False), 1,
            [SCALARS, pl.BlockSpec((1, DI // 2, D), lambda i: (layer, 0, 0))],
            whole((DI // 4, D)), struct((DI // 4, D), BF16), [], "take", deps,
        )(offs, reduce_weight)

    first_taken = take_lanes(0, DI, US, ())

    def fetch_layer(layer, after_near=(), after_far=(), after_rows=()):
        near = first_taken if layer == 0 else take_lanes(layer, DI, US, after_near)
        far = take_lanes(layer, 0, DI, after_far + (near,))
        rows_of = take_rows(layer, after_rows + (far,))
        return fetch(near), fetch(far), fetch(rows_of)

    weights = [fetch_layer(0)]

    resid = gather_tokens(following(tokens, first_taken)).astype(F32)
    grad = gather_tokens(cotangent).astype(F32)
    saved, out_both = [], ()
    for layer in range(LAYERS):
        near, far, rows_of = weights[layer]
        us, normed = expand_first(offs, resid, norm_all[layer][None], expand_t, near, layer)
        rim = us[T - 8 :, :CH]
        rim = next_piece(following(rim, far[0]) if layer else rim)
        taps, heads = taps_all[layer], heads_all[layer]
        skip = skip_rows[layer][None]
        act, slope, aux, lt, drow, sout, msg = ssd_front(us, rim, segx, taps, heads, hot_t, copies, out_both[1:])
        z = expand_rest(offs, normed, expand_t, far, layer, (act,))
        s_in, decays = carry_forward(core, following(msg, rows_of[0]) if layer else msg)
        normed_both = normed, swap(normed, "core")
        within_deps = (normed_both[1], grad) if layer else normed_both[1:]
        yloc = ssd_within(act, aux, lt, segx, segr, sout, skip, within_deps)
        if layer + 1 < LAYERS:
            weights.append(fetch_layer(layer + 1, (us,), (act,), (yloc,)))
        gain = gate_all[layer][None]
        y, out_mine, out_other, resid_next = ssd_gate(
            wide_offs, yloc, aux, drow, s_in, act, z, gain, resid, reduce_weight, rows_of, layer
        )
        out_both = out_mine, swap(out_other, "core")
        saved.append((resid, normed_both, z, us, rim, act, slope, aux, lt, drow, sout, s_in, decays, y, out_both))
        resid = resid_next
    layer_out = scatter_tokens(resid.astype(BF16))

    small = [None] * LAYERS
    far_sums, near_sums, pending = {}, {}, ()

    for layer in reversed(range(LAYERS)):
        near, far, rows_of = weights[layer]
        (resid_in, normed_both, z, us, rim, act, slope, aux, lt, drow, sout, s_in, decays, y, out_both) = saved[layer]
        taps, heads = taps_all[layer], heads_all[layer]
        skip = skip_rows[layer][None]
        gain = gate_all[layer][None]
        first = layer == 0
        dy, dy_rest, dzm, dzo, ggrad, zloc, gmsg, dsuf, grad_low = gate_back(
            wide_offs, grad, y, z, gain, act, aux, drow, reduce_weight, rows_of, layer, pending
        )
        arrived = near_sums[1].cross((gmsg,)) if first else ()
        zdev = carry_backward(core, following(gmsg, *arrived), decays)
        far_args = (dzm, swap(dzo, "core"), *normed_both, *out_both, grad_low, swap(grad_low, "core"))
        far_sums[layer] = Sum(offs, "far_grads", far_grads_kernel, far_args, FAR_MID, arrived)
        before = (far_sums[layer].own,)
        if first:
            before += near_sums[1].meet((zdev,) + before)
        dxs, dbc = within_back(act, aux, lt, segx, segr, dy, dy_rest, sout, drow, s_in, zloc, before)
        before = far_sums[layer].cross((dxs,))
        if first:
            before += (far_sums[1].mine,) + near_sums[1].reduce((dxs,))
        dum, duo, tail, rimout, tgrad, hgrad = ssd_last(
            offs, act, aux, slope, us, rim, segx, taps, heads, skip, hot, copies, dy, y, dxs, dbc, sout, drow, s_in,
            zloc, dsuf, zdev, before
        )
        token = far_sums[layer].meet((dum,)) + ((near_sums[1].mine,) if first else (layer_out[0],))
        rimout = following(rimout, *token)
        tail = (tail + next_piece(rimout, True).astype(F32)).astype(BF16)
        tail_mine, tail_other = halves(tail, core, 1)
        dum = lax.dynamic_update_slice(dum, tail_mine, (T - 8, 0))
        duo = lax.dynamic_update_slice(duo, tail_other, (T - 8, 0))
        near_args = (dum, swap(duo, "core"), *normed_both)
        grad, ngrad = input_back(
            offs, dzm, dzo, dum, duo, norm_all[layer][None], resid_in, grad, expand_t, near, far, layer, token
        )
        near_sums[layer] = Sum(offs, "near_grads", near_grads_kernel, near_args, NEAR_MID, (grad,))
        if not first:
            pending = far_sums[1].reduce((near_sums[1].own,))
        tgrad = jnp.sum(tgrad.reshape(5, 8, CH), axis=1).reshape(-1)
        hgrad = jnp.sum(hgrad.reshape(3, 8, LANES), axis=1)[:, :H].reshape(-1)
        small[layer] = jnp.concatenate([tgrad, jnp.sum(ggrad, axis=0), jnp.sum(ngrad, axis=0), hgrad])

    size = small[0].shape[0]
    padded_size = -(-size // 1024) * 1024
    packed = jnp.pad(jnp.stack(small), ((0, 0), (0, padded_size - size))).reshape(-1, LANES)
    hops = [("core", 1), ("fsdp", 1)] + levels()

    def hop(packed):
        axis, bit = hops.pop(0)
        return packed + flip(packed, axis, bit)

    far_other = swap(far_sums[1].mine, "rep")
    token = far_sums[0].reduce((near_sums[0].own, far_other))
    packed = hop(packed)
    token = near_sums[0].cross(token + (packed,))
    near_other = swap(near_sums[1].mine, "rep")
    packed = hop(packed)
    token = near_sums[0].meet(token + (far_sums[0].mine, near_other, packed))
    mid = far_sums[0].mine.shape[0] // 2
    other_a = swap(far_sums[0].mine[:mid], "rep")
    grads = final_grads(offs, far_sums[1].spread(far_other), near_sums[1].spread(near_other), 1, (), token)
    packed = hop(packed)
    token = near_sums[0].reduce(token + (other_a, packed, grads[0]))
    other_b = swap(far_sums[0].mine[mid:], "rep")
    packed = hop(packed)
    token_grads = scatter_tokens(following(grad.astype(BF16), near_sums[0].mine))
    far_first = far_sums[0].spread(jnp.concatenate([other_a, other_b], axis=0))
    while hops:
        packed = hop(packed)
    grads = final_grads(offs, far_first, near_sums[0].spread(), 0, grads)
    packed = packed.reshape(LAYERS, padded_size)

    def own_half(x):
        return halves(x, fsdp, x.ndim - 1)[0]

    tap_grads = own_half(packed[:, : 4 * CH].reshape(LAYERS, 4, CH))
    offset_grads = own_half(packed[:, 4 * CH : 5 * CH])
    at = 5 * CH
    gating_grads = own_half(packed[:, at : at + DI])
    at += DI
    norm_grads = own_half(packed[:, at : at + D])
    at += D
    step_grads = own_half(packed[:, at : at + H])
    decay_grads = own_half(packed[:, at + H : at + 2 * H])
    skip_grads = own_half(packed[:, at + 2 * H : at + 3 * H])

    return (
        layer_out,
        token_grads,
        jnp.swapaxes(grads[0], 1, 2),
        grads[1],
        tap_grads,
        offset_grads,
        step_grads,
        decay_grads,
        skip_grads,
        norm_grads,
        gating_grads,
    )


def solution(mesh):
    rep, fsdp, ctx = (mesh.shape[name] for name in ("rep", "fsdp", "ctx"))
    inner = Mesh(mesh.devices.reshape(rep, fsdp, ctx // 2, 2), ("rep", "fsdp", "zz", "core"))
    tokens = P(("rep", "fsdp"), ("zz", "core"), None)
    first, last = P(None, "fsdp"), P(None, None, "fsdp")
    return jax.shard_map(
        local,
        mesh=inner,
        in_specs=(
            tokens, P(("rep", "fsdp"), None), P(None, "fsdp", None), P(None, "fsdp", None), last,
            first, first, first, first, first, first, tokens,
        ),
        out_specs=(
            tokens, tokens, P(None, "fsdp", None), P(None, "fsdp", None), last,
            first, first, first, first, first, first,
        ),
        check_vma=False,
    )
```

```python
import functools

import jax
import jax.numpy as jnp
from jax import lax
from jax.experimental import pallas as pl
from jax.experimental.pallas import tpu as pltpu
from jax.sharding import Mesh, PartitionSpec as P

H = 32
P_SIZE = 64
N = 128
CONV = 4
LAYERS = 2
DI = 2048
CH = 2304
D = 1024
EPSILON = 1e-05
Q = 128
LANES = 128
PAIRS = DI // LANES
BLOCKS = CH // LANES
KEYS, READS, KEYS_REST, READS_REST = (slice(DI + i * N, DI + (i + 1) * N) for i in range(4))
ACT = DI + 4 * N
E = DI + CH + H
US = CH + H
HALF = CH // 2 + LANES
WIDE = 512
FAR_MID, NEAR_MID = DI // 2, 768
FAR = -1e30
F32 = jnp.float32
BF16 = jnp.bfloat16
VMEM_LIMIT = 56 * 1024 * 1024


def dot_nn(a, b):
    return lax.dot_general(a, b, (((1,), (0,)), ((), ())), preferred_element_type=F32)


def dot_nt(a, b):
    return lax.dot_general(a, b, (((1,), (1,)), ((), ())), preferred_element_type=F32)


def dot_tn(a, b):
    return lax.dot_general(a, b, (((0,), (0,)), ((), ())), preferred_element_type=F32)


def dot_full(a, b):
    return lax.dot_general(
        a, b, (((1,), (0,)), ((), ())), precision=lax.Precision.HIGHEST, preferred_element_type=F32
    )


def two_parts(x):
    high = x.astype(BF16)
    return high, (x - high.astype(F32)).astype(BF16)


def low_lanes():
    return lax.broadcasted_iota(jnp.int32, (Q, LANES), 1) < P_SIZE


def spread(table, first, pair, low):
    a = table[:, first + 2 * pair : first + 2 * pair + 1]
    b = table[:, first + 2 * pair + 1 : first + 2 * pair + 2]
    return jnp.where(low, a, b)


def column(table, index):
    return table[:, index : index + 1]


def lanes_of(index):
    return pl.ds(index * LANES, LANES)


def fold_rows(x):
    return jnp.sum(x.reshape(x.shape[0] // 8, 8, x.shape[1]), axis=0)


STEP, LOGS, TO_END, FROM_START = 0, 32, 64, 96


def front_kernel(
    us_ref, rim_ref, segx_ref, taps_ref, heads_ref, oht_ref, copies_ref,
    act_ref, slope_ref, aux_ref, lt_ref, drow_ref, sout_ref, msg_ref,
    ubuf, state, decay, xbuf,
):
    c = pl.program_id(0)

    @pl.when(c == 0)
    def _():
        ubuf[0:8, :] = rim_ref[...].astype(F32)
        state[...] = jnp.zeros_like(state)
        decay[...] = jnp.ones_like(decay)

    @pl.when(c > 0)
    def _():
        ubuf[0:8, :] = ubuf[Q : Q + 8, :]

    seg_rows = segx_ref[pl.ds(pl.multiple_of(c * Q, Q), Q + 8), :]
    seg = seg_rows[8:]
    masks = [(seg_rows[5 + k : 5 + k + Q] == seg).astype(F32) for k in range(CONV - 1)]
    for j in range(BLOCKS):
        cols = lanes_of(j)
        ubuf[8 : 8 + Q, cols] = us_ref[:, cols].astype(F32)
        filtered = taps_ref[4:5, cols] + taps_ref[3:4, cols] * ubuf[8 : 8 + Q, cols]
        for k in range(CONV - 1):
            filtered += taps_ref[k : k + 1, cols] * (ubuf[5 + k : 5 + k + Q, cols] * masks[k])
        gate = 1.0 / (1.0 + jnp.exp(-filtered))
        active = filtered * gate
        act_ref[:, cols] = active.astype(BF16)
        if j >= PAIRS:
            act_ref[:, lanes_of(j + 2)] = two_parts(active)[1]
        slope_ref[:, cols] = (gate * (1.0 + filtered - active)).astype(BF16)

    raw = dot_nn(us_ref[:, CH:], copies_ref[...]) + heads_ref[0:1, :]
    step = jnp.maximum(raw, 0.0) + jnp.log1p(jnp.exp(-jnp.abs(raw)))
    rows = lax.broadcasted_iota(jnp.int32, (Q, Q), 0)
    lane = lax.broadcasted_iota(jnp.int32, (Q, Q), 1)
    logs = dot_full((rows >= lane).astype(F32), -(step * heads_ref[1:2, :]))
    last = logs[Q - 1 : Q, :]
    joined = (seg_rows[8:9] == seg_rows[7:8]).astype(F32)
    to_end = jnp.exp(last - logs) * (seg == seg[Q - 1 : Q]).astype(F32)
    from_start = jnp.exp(logs) * (joined * (seg == seg[0:1]).astype(F32))
    aux = jnp.where(
        lane < 64, jnp.where(lane < 32, step, logs), jnp.where(lane < 96, to_end, from_start)
    )
    aux_ref[...] = aux
    lt_ref[0] = logs.T[:H, :]
    through = jnp.exp(last) * joined * (seg[Q - 1 : Q] == seg[0:1]).astype(F32)
    before = decay[0:1, :]
    after = before * through
    row16 = lax.broadcasted_iota(jnp.int32, (16, LANES), 0)
    table = jnp.where(row16 == 0, through, jnp.where(row16 == 1, before, after))
    high, rest = two_parts(table)
    drow = dot_nn(high, oht_ref[...]) + dot_nn(rest, oht_ref[...])
    drow_ref[0] = drow[0:8]
    decay[...] = jnp.broadcast_to(after, decay.shape)

    low = low_lanes()
    for j in range(PAIRS):
        scaled = (spread(aux, STEP, j, low) * act_ref[:, lanes_of(j)].astype(F32)).astype(BF16)
        xbuf[:, lanes_of(j)] = (spread(aux, TO_END, j, low) * scaled.astype(F32)).astype(BF16)
    keys = act_ref[:, KEYS].astype(F32).T.astype(BF16)
    held = state[...] * drow[0:1, :] + dot_nn(keys, xbuf[...])
    state[...] = held
    sout_ref[0] = held
    msg_ref[0:N, :] = held
    msg_ref[N : N + 8, :] = jnp.broadcast_to(drow[2:3], (8, DI))


def within_kernel(act_ref, aux_ref, lt_ref, segx_ref, segr_ref, sprev_ref, skip_ref, y_ref):
    c = pl.program_id(0)
    seg = segx_ref[pl.ds(pl.multiple_of(c * Q + 8, 8), Q), :]
    rows = lax.broadcasted_iota(jnp.int32, (Q, Q), 0)
    lane = lax.broadcasted_iota(jnp.int32, (Q, Q), 1)
    bias = jnp.where((rows >= lane) & (seg == segr_ref[0, 0:1, :]), 0.0, FAR)
    reads = act_ref[:, READS]
    reads_both = jnp.concatenate([reads, act_ref[:, READS_REST]], axis=1)
    keys_twice = jnp.concatenate([act_ref[:, KEYS]] * 2, axis=1)
    scores = dot_nt(reads_both, keys_twice) + dot_nt(reads, act_ref[:, KEYS_REST])
    aux = aux_ref[...]
    low = low_lanes()
    has_prev = (c > 0).astype(F32)
    for j in range(PAIRS):
        cols = lanes_of(j)
        weights = [
            (jnp.exp(column(aux, LOGS + h) - lt_ref[0, h : h + 1, :] + bias) * scores).astype(BF16)
            for h in (2 * j, 2 * j + 1)
        ]
        values = act_ref[:, cols].astype(F32)
        scaled = spread(aux, STEP, j, low) * values
        stack = jnp.concatenate(
            [jnp.where(low, scaled, 0.0), jnp.where(low, 0.0, scaled)], axis=0
        ).astype(BF16)
        high, rest = two_parts(sprev_ref[0, :, cols])
        carried = dot_nn(reads_both, jnp.concatenate([high, high], axis=0)) + dot_nn(reads, rest)
        carried *= spread(aux, FROM_START, j, low) * has_prev
        y_ref[:, cols] = (
            dot_nn(jnp.concatenate(weights, axis=1), stack)
            + carried
            + skip_ref[0:1, cols] * values
        )


def gate_kernel(
    offs_ref, yloc_ref, aux_ref, drow_ref, sin_ref, reads_ref, rest_ref, z_ref, gain_ref, resid_ref,
    own_ref, *others
):
    pieces, (y_ref, mine_ref, other_ref, next_ref, gbuf, obuf) = others[:-6], others[-6:]
    i = pl.program_id(0)
    aux = aux_ref[...]
    reads = reads_ref[...]
    reads_both = jnp.concatenate([reads, rest_ref[...]], axis=1)
    low = low_lanes()
    total = jnp.zeros((Q, LANES), F32)
    for j in range(PAIRS):
        cols = lanes_of(j)
        high, rest = two_parts(sin_ref[:, cols])
        carried = dot_nn(reads_both, jnp.concatenate([high, high], axis=0)) + dot_nn(reads, rest)
        y = yloc_ref[:, cols] + carried * (spread(aux, FROM_START, j, low) * drow_ref[0, 1:2, cols])
        y_ref[:, cols] = y
        z = z_ref[:, cols].astype(F32)
        gated = y * (z / (1.0 + jnp.exp(-z)))
        gbuf[:, cols] = gated
        total += gated * gated
    scale = lax.rsqrt(jnp.sum(total, axis=1, keepdims=True) * (1.0 / DI) + EPSILON)
    rows = pl.ds(pl.multiple_of(i * Q, Q), Q)
    for j in range(PAIRS):
        cols = lanes_of(j)
        obuf[rows, cols] = (gbuf[:, cols] * scale * gain_ref[0:1, cols]).astype(BF16)

    @pl.when(i == pl.num_programs(0) - 1)
    def _():
        half, quarter = DI // 2, DI // 4
        core = offs_ref[7]

        def taken(start, width):
            return obuf[:, pl.ds(pl.multiple_of(start, quarter), width)]

        for k, start in enumerate((offs_ref[0], half - offs_ref[0])):
            cols = slice(k * quarter, (k + 1) * quarter)
            mine_ref[:, cols] = taken(start + core * quarter, quarter)
            other_ref[:, cols] = taken(start + (1 - core) * quarter, quarter)
        left = jnp.concatenate(
            [taken(offs_ref[0], half)] + [taken(offs_ref[k + 1], quarter) for k in range(len(pieces))], axis=1
        )
        for j in range(D // 256):
            cols = pl.ds(j * 256, 256)
            right = jnp.concatenate([own_ref[0, :, cols]] + [p[:, cols] for p in pieces], axis=0)
            next_ref[:, cols] = resid_ref[:, cols] + dot_nn(left, right)


def gate_back_kernel(
    offs_ref, grad_ref, y_ref, z_ref, gain_ref, reads_ref, aux_ref, drow_ref, own_ref, *others
):
    pieces, others = others[:-15], others[-15:]
    (dy_ref, rest_ref, dzm_ref, dzo_ref, ggrad_ref, zloc_ref, gmsg_ref, dsuf_ref, low_ref,
     gbuf, grad_state, suffix, xbuf, dout, zbuf) = others
    i = pl.program_id(0)

    @pl.when(i == 0)
    def _():
        low_ref[...] = grad_ref[...].astype(BF16)
        left = low_ref[...]
        for j in range(DI // 512):
            right = own_ref[0, 256 * j : 256 * (j + 1), :]
            cols = pl.ds(pl.multiple_of(offs_ref[0] + 256 * j, 256), 256)
            dout[:, cols] = dot_nt(left, right)
        quarter = DI // 4
        for k, p in enumerate(pieces):
            for j in range(quarter // 256):
                right = p[256 * j : 256 * (j + 1), :]
                cols = pl.ds(pl.multiple_of(offs_ref[k + 1] + 256 * j, 256), 256)
                dout[:, cols] = dot_nt(left, right)
        ggrad_ref[...] = jnp.zeros_like(ggrad_ref)
        grad_state[...] = jnp.zeros_like(grad_state)
        suffix[...] = jnp.ones_like(suffix)

    rows = pl.ds(pl.multiple_of((pl.num_programs(0) - 1 - i) * Q, Q), Q)
    aux = aux_ref[...]
    low = low_lanes()
    total = jnp.zeros((Q, LANES), F32)
    cross = jnp.zeros((Q, LANES), F32)
    for j in range(PAIRS):
        cols = lanes_of(j)
        z = z_ref[:, cols].astype(F32)
        gated = y_ref[:, cols] * (z / (1.0 + jnp.exp(-z)))
        gbuf[:, cols] = gated
        total += gated * gated
        cross += gated * (dout[rows, cols] * gain_ref[0:1, cols])
    scale = lax.rsqrt(jnp.sum(total, axis=1, keepdims=True) * (1.0 / DI) + EPSILON)
    pull = jnp.sum(cross, axis=1, keepdims=True) * (scale * scale * scale * (1.0 / DI))
    scale = jnp.broadcast_to(scale, (Q, LANES))
    pull = jnp.broadcast_to(pull, (Q, LANES))
    for j in range(PAIRS):
        cols = lanes_of(j)
        z = z_ref[:, cols].astype(F32)
        gate = 1.0 / (1.0 + jnp.exp(-z))
        gated = gbuf[:, cols]
        scaled = dout[rows, cols] * scale
        ggrad_ref[:, cols] += fold_rows(scaled * gated)
        d_gated = scaled * gain_ref[0:1, cols] - gated * pull
        dy, rest = two_parts(d_gated * (z * gate))
        dy_ref[:, cols] = dy
        rest_ref[:, cols] = rest
        zbuf[:, cols] = (d_gated * y_ref[:, cols] * (gate * (1.0 + z * (1.0 - gate)))).astype(BF16)
        xbuf[:, cols] = (dy.astype(F32) * spread(aux, FROM_START, j, low)).astype(BF16)
    half, core = DI // 2, offs_ref[7]
    dzm_ref[...] = zbuf[:, pl.ds(pl.multiple_of(core * half, half), half)]
    dzo_ref[...] = zbuf[:, pl.ds(pl.multiple_of((1 - core) * half, half), half)]
    zloc_ref[0] = grad_state[...].astype(BF16)
    dsuf_ref[0] = suffix[...]
    reads = reads_ref[...].astype(F32).T.astype(BF16)
    through = drow_ref[0, 0:1, :]
    grad_state[...] = grad_state[...] * through + dot_nn(reads, xbuf[...])
    suffix[...] = suffix[...] * through
    gmsg_ref[...] = grad_state[...].astype(BF16)


def within_back_kernel(
    act_ref, aux_ref, lt_ref, segx_ref, segr_ref, dy_ref, rest_ref, sprev_ref, drow_ref, sin_ref, zloc_ref,
    dxs_ref, dbc_ref, wbuf, wrest, ibuf, irest, ebuf,
):
    c = pl.program_id(0)
    seg = segx_ref[pl.ds(pl.multiple_of(c * Q + 8, 8), Q), :]
    rows = lax.broadcasted_iota(jnp.int32, (Q, Q), 0)
    lane = lax.broadcasted_iota(jnp.int32, (Q, Q), 1)
    bias = jnp.where((rows <= lane) & (seg == segr_ref[0, 0:1, :]), 0.0, FAR)
    keys, reads = act_ref[:, KEYS], act_ref[:, READS]
    scores = dot_nt(
        jnp.concatenate([keys, keys], axis=1), jnp.concatenate([reads, act_ref[:, READS_REST]], axis=1)
    ) + dot_nt(act_ref[:, KEYS_REST], reads)
    aux = aux_ref[...]
    low = low_lanes()
    has_prev = (c > 0).astype(F32)
    d_scores = jnp.zeros((Q, Q), F32)
    for j in range(PAIRS):
        cols = lanes_of(j)
        fades = [
            jnp.exp(lt_ref[0, h : h + 1, :] - column(aux, LOGS + h) + bias)
            for h in (2 * j, 2 * j + 1)
        ]
        weights = jnp.concatenate([(fade * scores).astype(BF16) for fade in fades], axis=1)
        dy = dy_ref[:, cols]
        dy_wide = dy.astype(F32)
        dy_rest = rest_ref[:, cols]
        stack = jnp.concatenate(
            [jnp.where(low, dy_wide, 0.0), jnp.where(low, 0.0, dy_wide)], axis=0
        ).astype(BF16)
        scaled = (spread(aux, STEP, j, low) * act_ref[:, cols].astype(F32)).astype(BF16).astype(F32)
        both = jnp.concatenate(
            [jnp.where(low, scaled, 0.0), jnp.where(low, 0.0, scaled)], axis=0
        ).astype(BF16)
        d_weights = dot_nt(
            jnp.concatenate([both, both], axis=1), jnp.concatenate([dy, dy_rest], axis=1)
        )
        d_scores += d_weights[:Q] * fades[0] + d_weights[Q:] * fades[1]
        to_end = spread(aux, TO_END, j, low)
        dxs_ref[:, cols] = dot_nn(weights, stack) + to_end * dot_nn(keys, zloc_ref[0, :, cols])
        wbuf[:, cols], wrest[:, cols] = two_parts(
            (dy_wide + dy_rest.astype(F32)) * spread(aux, FROM_START, j, low)
        )
        ebuf[:, cols] = (to_end * scaled).astype(BF16)
        ibuf[:, cols], irest[:, cols] = two_parts(
            drow_ref[0, 1:2, cols] * sin_ref[:, cols] + has_prev * sprev_ref[0, :, cols]
        )
    dbc_ref[:, 0:N] = dot_nn(d_scores.astype(BF16), reads) + dot_nt(ebuf[...], zloc_ref[0])
    high, rest = two_parts(d_scores.T)
    dbc_ref[:, N:] = (
        dot_nn(high, keys)
        + dot_nn(rest, keys)
        + dot_nt(wbuf[...], ibuf[...])
        + dot_nt(wrest[...], ibuf[...])
        + dot_nt(wbuf[...], irest[...])
    )


def last_kernel(
    offs_ref, act_ref, aux_ref, slope_ref, us_ref, rim_ref, segx_ref, taps_ref, heads_ref, skip_ref,
    oh_ref, copies_ref, dy_ref, y_ref, dxs_ref, dbc_ref, sout_ref, drow_ref, sin_ref, zloc_ref, dsuf_ref, zdev_ref,
    dum_ref, duo_ref, tail_ref, rimout_ref, tgrad_ref, hgrad_ref,
    dubuf, dbuf, qhigh, qrest, vbuf, ebuf, sums, skips,
):
    i = pl.program_id(0)
    count = pl.num_programs(0)
    c = count - 1 - i

    @pl.when(i == 0)
    def _():
        dbuf[Q : Q + 8, :] = jnp.zeros((8, CH), F32)
        tgrad_ref[...] = jnp.zeros_like(tgrad_ref)
        hgrad_ref[...] = jnp.zeros_like(hgrad_ref)
        skips[...] = jnp.zeros_like(skips)

    @pl.when(i > 0)
    def _():
        dbuf[Q : Q + 8, :] = dbuf[0:8, :]

    aux = aux_ref[...]
    low = low_lanes()
    keys = act_ref[:, KEYS]
    for j in range(PAIRS):
        cols = lanes_of(j)
        dy = dy_ref[:, cols].astype(F32)
        values = act_ref[:, cols].astype(F32)
        step = spread(aux, STEP, j, low)
        scaled = (step * values).astype(BF16).astype(F32)
        reach = spread(aux, TO_END, j, low) * dsuf_ref[0, 0:1, cols]
        dxs = dxs_ref[:, cols] + reach * dot_nn(keys, zdev_ref[:, cols])
        ebuf[:, cols] = (reach * scaled).astype(BF16)
        skip = skip_ref[0:1, cols]
        dbuf[0:Q, cols] = (step * dxs + skip * dy) * slope_ref[:, cols].astype(F32)
        qhigh[:, cols], qrest[:, cols] = two_parts(dy * (y_ref[:, cols] - skip * values) - scaled * dxs)
        vbuf[:, cols] = (values * dxs).astype(BF16)
        skips[:, cols] += fold_rows(values * dy)
        arrived = zloc_ref[0, :, cols].astype(F32) + dsuf_ref[0, 0:1, cols] * zdev_ref[:, cols].astype(F32)
        leaving = sout_ref[0, :, cols] + drow_ref[0, 2:3, cols] * sin_ref[:, cols]
        sums[:, cols] = jnp.sum((arrived * leaving).reshape(N // 16, 16, LANES), axis=0)
    d_keys = dbc_ref[:, 0:N] + dot_nt(ebuf[...], zdev_ref[...])
    dbuf[0:Q, DI : DI + N] = d_keys * slope_ref[:, DI : DI + N].astype(F32)
    dbuf[0:Q, DI + N :] = dbc_ref[:, N:] * slope_ref[:, DI + N :].astype(F32)

    hot = oh_ref[...]

    def by_head(x):
        high, rest = two_parts(x)
        return dot_nn(high, hot) + dot_nn(rest, hot)

    stacked = jnp.concatenate([qhigh[...], qrest[...], vbuf[...], *two_parts(sums[...])], axis=0)
    head_sums = dot_nn(stacked, hot)
    d_logs = head_sums[:Q] + head_sums[Q : 2 * Q]
    d_last = jnp.sum(head_sums[3 * Q :], axis=0, keepdims=True)
    rows = lax.broadcasted_iota(jnp.int32, (Q, Q), 0)
    lane = lax.broadcasted_iota(jnp.int32, (Q, Q), 1)
    d_decay = dot_full((rows <= lane).astype(F32), d_logs) + d_last
    raw = dot_nn(us_ref[:, CH:], copies_ref[...]) + heads_ref[0:1, :]
    step = jnp.maximum(raw, 0.0) + jnp.log1p(jnp.exp(-jnp.abs(raw)))
    d_step = head_sums[2 * Q : 3 * Q] - heads_ref[1:2, :] * d_decay
    d_raw = d_step / (1.0 + jnp.exp(-raw))
    d_raw = jnp.where(lane < H, d_raw, 0.0)
    dum_ref[:, CH // 2 :] = d_raw.astype(BF16)
    duo_ref[:, CH // 2 :] = d_raw.astype(BF16)
    hgrad_ref[0:8, :] += fold_rows(d_raw)
    hgrad_ref[8:16, :] += fold_rows(-(step * d_decay))

    @pl.when(i == count - 1)
    def _():
        hgrad_ref[16:24, :] = by_head(skips[...])

    seg_rows = segx_ref[pl.ds(pl.multiple_of(c * Q + 8, 8), Q + 8), :]
    seg = seg_rows[:Q]
    masks = [(seg_rows[m : m + Q] == seg).astype(F32) for m in range(1, CONV)]
    for j in range(BLOCKS):
        cols = lanes_of(j)
        d_filtered = dbuf[0:Q, cols]
        u = us_ref[:, cols].astype(F32)
        du = taps_ref[3:4, cols] * d_filtered
        tgrad_ref[24:32, cols] += fold_rows(u * d_filtered)
        tgrad_ref[32:40, cols] += fold_rows(d_filtered)
        for m in range(1, CONV):
            later = dbuf[m : m + Q, cols] * masks[m - 1]
            du += taps_ref[3 - m : 4 - m, cols] * later
            tgrad_ref[8 * (3 - m) : 8 * (4 - m), cols] += fold_rows(u * later)
        dubuf[:, cols] = du.astype(BF16)

        @pl.when(i == 0)
        def _():
            tail_ref[:, cols] = du[Q - 8 :]

    half, core = CH // 2, offs_ref[7]
    dum_ref[:, :half] = dubuf[:, pl.ds(pl.multiple_of(core * half, LANES), half)]
    duo_ref[:, :half] = dubuf[:, pl.ds(pl.multiple_of((1 - core) * half, LANES), half)]

    @pl.when(i == count - 1)
    def _():
        near = segx_ref[0:16, :]
        rim_masks = [(near[m : m + 8] == near[0:8]).astype(F32) for m in range(1, CONV)]
        for j in range(BLOCKS):
            cols = lanes_of(j)
            edge = jnp.concatenate([jnp.zeros((8, LANES), F32), dbuf[0:8, cols]], axis=0)
            u = rim_ref[:, cols].astype(F32)
            out = jnp.zeros((8, LANES), F32)
            for m in range(1, CONV):
                later = edge[m : m + 8] * rim_masks[m - 1]
                out += taps_ref[3 - m : 4 - m, cols] * later
                tgrad_ref[8 * (3 - m) : 8 * (4 - m), cols] += u * later
            rimout_ref[:, cols] = out.astype(BF16)


def expand_first_kernel(offs_ref, resid_ref, gain_ref, own_ref, *others):
    pieces, (out_ref, normed_ref, left) = others[:-3], others[-3:]
    half = D // 2

    @pl.when(pl.program_id(0) == 0)
    def _():
        x = resid_ref[...]
        scale = lax.rsqrt(jnp.mean(x * x, axis=1, keepdims=True) + EPSILON)
        left[...] = (x * scale * gain_ref[...]).astype(BF16)
        own = left[:, pl.ds(pl.multiple_of(offs_ref[0], half), half)]
        normed_ref[:, half:] = left[:, pl.ds(pl.multiple_of(half - offs_ref[0], half), half)]
        normed_ref[:, :half] = own

    out_ref[...] = expand_block(offs_ref, normed_ref, own_ref, pieces).astype(BF16)


def expand_block(offs_ref, normed_ref, own_ref, pieces):
    half = D // 2
    parts = [normed_ref[:, :half]]
    for k, p in enumerate(pieces):
        at = half + lax.rem(offs_ref[k + 1], half)
        parts.append(normed_ref[:, pl.ds(pl.multiple_of(at, LANES), p.shape[1])])
    right = jnp.concatenate([own_ref[0]] + [p[...] for p in pieces], axis=1)
    return dot_nt(jnp.concatenate(parts, axis=1), right)


def expand_rest_kernel(offs_ref, normed_ref, own_ref, *others):
    pieces, out_ref = others[:-1], others[-1]
    out_ref[...] = expand_block(offs_ref, normed_ref, own_ref, pieces).astype(BF16)


def input_back_kernel(
    count, layer, offs_ref, dzm_ref, dzo_ref, dum_ref, duo_ref, gain_ref, resid_ref, grad_ref, own_ref, *others
):
    near, far = others[:count], others[count : 2 * count]
    (next_ref, ngrad_ref, own, *bufs), (dn, sems) = others[2 * count : -2], others[-2:]
    near_bufs, far_bufs = bufs[:count], bufs[count:]
    moves = [(own_ref.at[layer], own)] + list(zip(near, near_bufs))
    moves += list(zip(far, far_bufs))
    copies = [pltpu.make_async_copy(src, dst, sems.at[k]) for k, (src, dst) in enumerate(moves)]
    for copy in copies:
        copy.start()
    copies[0].wait()
    core, zs, us = offs_ref[7], DI // 2, CH // 2
    parts = [
        (dzm_ref[...], 0, core * zs), (dzo_ref[...], 0, (1 - core) * zs),
        (dum_ref[:, :us], DI, core * us), (duo_ref[:, :us], DI, (1 - core) * us), (dum_ref[:, us : us + H], DI + CH, 0),
    ]

    def down(part, buf, base):
        left, start, at = part
        if not isinstance(at, int):
            at = pl.multiple_of(at, LANES)
        return dot_nn(left, buf[pl.ds(start - base + at, left.shape[1]), base_cols])

    for j in range(D // 2 // 256):
        base_cols = slice(j * 256, (j + 1) * 256)
        cols = pl.ds(pl.multiple_of(offs_ref[0] + j * 256, 256), 256)
        dn[:, cols] = sum(down(part, own, 0) for part in parts)
    base_cols = slice(None)
    for k in range(count):
        copies[1 + k].wait()
        copies[1 + count + k].wait()
        cols = pl.ds(pl.multiple_of(offs_ref[k + 1], LANES), near_bufs[k].shape[1])
        dn[:, cols] = sum(down(part, far_bufs[k], 0) for part in parts[:2]) + sum(
            down(part, near_bufs[k], DI) for part in parts[2:]
        )
    ngrad = jnp.zeros((8, D), F32)
    for i in range(dzm_ref.shape[0] // Q):
        rows = slice(i * Q, (i + 1) * Q)
        x = resid_ref[rows, :]
        scale = lax.rsqrt(jnp.mean(x * x, axis=1, keepdims=True) + EPSILON)
        unit = x * scale
        down = dn[rows, :]
        ngrad += fold_rows(down * unit)
        pulled = down * gain_ref[...]
        mean = jnp.mean(pulled * unit, axis=1, keepdims=True)
        next_ref[rows, :] = grad_ref[rows, :] + scale * (pulled - unit * mean)
    ngrad_ref[...] = ngrad


def rows_at(which, size, base=0):
    return pl.ds(pl.multiple_of(base + which * size, 16), size)


def weight_grads(i, count, offs_ref, left, right, away_left, away_right, own_ref, away_ref, near_ref, far_ref):
    size, width = own_ref.shape
    first = near_ref.shape[0] // size
    mine = dot_tn(left, right).astype(BF16)
    away = dot_tn(away_left, away_right).astype(BF16)
    own_ref[...] = mine
    away_ref[...] = away

    @pl.when(i < first)
    def _():
        near_ref[rows_at(i, size), :] = away

    start = first + (1 - offs_ref[6]) * (far_ref.shape[0] // size)

    @pl.when((i >= start) & (i < start + far_ref.shape[0] // size))
    def _():
        far_ref[rows_at(i - start, size), :width] = mine
        far_ref[rows_at(i - start, size), width:] = away


def both_of(pair, lanes):
    return jnp.concatenate([ref[:, lanes] for ref in pair], axis=0)


def far_grads_kernel(offs_ref, dzm, dzr, nm, nr, om, orr, lm, lr, *outs):
    i = pl.program_id(0)
    half, size = D // 2, 256

    @pl.when(i < 4)
    def _():
        left = both_of((dzm, dzr), pl.ds(pl.multiple_of(i * size, size), size))
        weight_grads(
            i, 8, offs_ref, left, both_of((nm, nr), slice(0, half)), left, both_of((nm, nr), slice(half, D)), *outs
        )

    @pl.when(i >= 4)
    def _():
        at = lax.rem(i, 2) * size
        right = both_of((lm, lr), pl.ds(pl.multiple_of((i - 4) // 2 * half, half), half))
        left = both_of((om, orr), pl.ds(pl.multiple_of(at, size), size))
        away = both_of((om, orr), pl.ds(pl.multiple_of(half + at, size), size))
        weight_grads(i, 8, offs_ref, left, right, away, right, *outs)


def near_grads_kernel(offs_ref, dum, dur, nm, nr, *outs):
    i = pl.program_id(0)
    half, size = D // 2, 256
    left = both_of((dum, dur), pl.ds(pl.multiple_of(i * size, size), size))
    weight_grads(
        i, 5, offs_ref, left, both_of((nm, nr), slice(0, half)), left, both_of((nm, nr), slice(half, D)), *outs
    )


def rows_at(which, size, base=0):
    return pl.ds(pl.multiple_of(base + which * size, LANES), size)


def cross_kernel(offs_ref, own_ref, away_ref, near_ref, far_ref, keep_ref, to_rep_ref, to_fsdp_ref):
    mid, width = near_ref.shape
    first, second, rep = to_rep_ref.shape[0], to_fsdp_ref.shape[0], offs_ref[6]
    for ref, which in ((keep_ref, rep), (to_rep_ref, 1 - rep)):
        rows = rows_at(which, first)
        total = own_ref[rows, :].astype(F32) + near_ref[rows, :].astype(F32)
        ref[:first, :] = total.astype(ref.dtype)
    rows = rows_at(rep, second, mid)
    keep_ref[first:, :] = own_ref[rows, :].astype(F32) + far_ref[:, :width].astype(F32)
    to_fsdp_ref[...] = (away_ref[rows, :].astype(F32) + far_ref[:, width:].astype(F32)).astype(BF16)


def meet_kernel(keep_ref, a_ref, b_ref, out_ref):
    size = a_ref.shape[0]
    out_ref[:size, :] = (keep_ref[:size, :] + a_ref[...].astype(F32)).astype(BF16)
    out_ref[size:, :] = (keep_ref[size:, :] + b_ref[...].astype(F32)).astype(BF16)


def take_kernel(lanes, offs_ref, src_ref, out_ref):
    rows, width = out_ref.shape
    core = offs_ref[7]
    if lanes:
        out_ref[...] = src_ref[0, :, pl.ds(pl.multiple_of(core * width, width), width)]
    else:
        out_ref[...] = src_ref[0, rows_at(core, rows), :]


def reduce_kernel(parts_ref, out_ref):
    count, rows = parts_ref.shape[0], parts_ref.shape[1]
    total = parts_ref[0].astype(F32)
    for k in range(1, count):
        total += parts_ref[k].astype(F32)
    total = total.astype(BF16)
    for k in range(count):
        out_ref[k * rows : (k + 1) * rows, :] = total


def placed(offs_ref, parts, mid, buf, k):
    for h, part in enumerate(parts):
        at = offs_ref[6] if h == 0 else 1 - offs_ref[6]
        size = mid // 2
        buf[k, rows_at(at, size), :] = part[:size, :].astype(F32)
        buf[k, rows_at(at, part.shape[0] - size, mid), :] = part[size:, :].astype(F32)


def send_all(layer, sems, moves):
    copies = []
    for src, ref, start, size in moves:
        copy = pltpu.make_async_copy(src, ref.at[layer, pl.ds(start, size)], sems.at[len(copies)])
        copy.start()
        copies.append(copy)
    for copy in copies:
        copy.wait()


def far_final_kernel(layer, offs_ref, *others):
    expand_ref, reduce_ref, zbuf, rbuf, sems = others[-5:]
    core, zs, rs = offs_ref[7], DI // 2, DI // 4
    moves = []
    for k in range(2):
        which = core if k == 0 else 1 - core
        placed(offs_ref, others[2 * k : 2 * k + 2], FAR_MID, zbuf, k)
        for q in range(2):
            rbuf[k, :, 512 * q : 512 * (q + 1)] = zbuf[k, zs + rs * q : zs + rs * (q + 1), :]
        moves.append((rbuf.at[k], reduce_ref, pl.multiple_of(which * rs, LANES), rs))
        moves.append((zbuf.at[k, pl.ds(0, zs)], expand_ref, pl.multiple_of(which * zs, LANES), zs))
    send_all(layer, sems, moves)


def near_final_kernel(layer, offs_ref, *others):
    expand_ref, ubuf, sems = others[-3:]
    core, us = offs_ref[7], CH // 2
    moves = []
    for k in range(2):
        which = core if k == 0 else 1 - core
        placed(offs_ref, others[2 * k : 2 * k + 2], NEAR_MID, ubuf, k)
        moves.append((ubuf.at[k, pl.ds(0, us)], expand_ref, pl.multiple_of(DI + which * us, LANES), us))
    moves.append((ubuf.at[0, pl.ds(us, H)], expand_ref, DI + CH, H))
    send_all(layer, sems, moves)


def whole(shape):
    return pl.BlockSpec(shape, lambda i: (0,) * len(shape))


def by_rows(shape, count=None):
    if count is None:
        return pl.BlockSpec(shape, lambda i: (i,) + (0,) * (len(shape) - 1))
    return pl.BlockSpec(shape, lambda i: (count - 1 - i,) + (0,) * (len(shape) - 1))


def struct(shape, dtype):
    return jax.ShapeDtypeStruct(shape, dtype)


SCALARS = pl.BlockSpec(memory_space=pltpu.SMEM)
ANYWHERE = pl.BlockSpec(memory_space=pl.ANY)


COST = {
    "expand_first": 8, "ssd_front": 13, "expand_rest": 6, "ssd_within": 11, "ssd_gate": 13, "gate_back": 15,
    "within_back": 17, "ssd_last": 24, "input_back": 16, "far_grads": 12, "near_grads": 6, "take": 1, "cross": 4, "meet": 3, "reduce_parts": 2,
    "far_final": 6, "near_final": 4,
}


def call(kernel, grid, in_specs, out_specs, out_shape, scratch, name, deps=(), aliases=None):
    n, m = len(in_specs), len(deps)

    def body(*refs):
        kernel(*refs[:n], *refs[n + m :])

    run = pl.pallas_call(
        body,
        grid=(grid,),
        in_specs=list(in_specs) + [ANYWHERE] * m,
        out_specs=out_specs,
        out_shape=out_shape,
        scratch_shapes=scratch,
        input_output_aliases=aliases or {},
        compiler_params=pltpu.CompilerParams(
            dimension_semantics=("arbitrary",), vmem_limit_bytes=VMEM_LIMIT
        ),
        cost_estimate=pl.CostEstimate(
            flops=int(COST[name] * 1.1e9), bytes_accessed=1000, transcendentals=0
        ),
        name=name,
    )
    return lambda *args: run(*args, *deps)


def expand_first(offs, resid, gain, own, pieces, layer):
    T = resid.shape[0]
    first = DI // WIDE
    return call(
        expand_first_kernel, -(-US // WIDE),
        [SCALARS, whole((T, D)), whole((1, D)),
         pl.BlockSpec((1, WIDE, D // 2), lambda i: (layer, first + i, 0))]
        + [pl.BlockSpec((WIDE, p.shape[1]), lambda i: (i, 0)) for p in pieces],
        [pl.BlockSpec((T, WIDE), lambda i: (0, i)), whole((T, D))],
        [struct((T, US), BF16), struct((T, D), BF16)],
        [pltpu.VMEM((T, D), BF16)],
        "expand_first",
    )(offs, resid, gain, own, *pieces)


def expand_rest(offs, normed, own, pieces, layer, deps=()):
    T = normed.shape[0]
    return call(
        expand_rest_kernel, DI // WIDE,
        [SCALARS, whole((T, D)), pl.BlockSpec((1, WIDE, D // 2), lambda i: (layer, i, 0))]
        + [pl.BlockSpec((WIDE, p.shape[1]), lambda i: (i, 0)) for p in pieces],
        pl.BlockSpec((T, WIDE), lambda i: (0, i)),
        struct((T, DI), BF16), [],
        "expand_rest", deps,
    )(offs, normed, own, *pieces)


def input_back(offs, dzm, dzo, dum, duo, gain, resid, grad, own, near, far, layer, deps=()):
    T = dzm.shape[0]
    count = len(near)
    return call(
        functools.partial(input_back_kernel, count, layer), 1,
        [SCALARS] + [whole(a.shape) for a in (dzm, dzo, dum, duo)]
        + [whole((1, D)), whole((T, D)), whole((T, D)), ANYWHERE] + [ANYWHERE] * (2 * count),
        [whole((T, D)), whole((8, D))],
        [struct((T, D), F32), struct((8, D), F32)],
        [pltpu.VMEM((E, D // 2), BF16)] + [pltpu.VMEM((US, p.shape[1]), BF16) for p in near]
        + [pltpu.VMEM((DI, p.shape[1]), BF16) for p in far]
        + [pltpu.VMEM((T, D), F32), pltpu.SemaphoreType.DMA((1 + 2 * count,))],
        "input_back", deps,
    )(offs, dzm, dzo, dum, duo, gain, resid, grad, own, *near, *far)


def far_final(offs, parts, layer, held, deps=()):
    n = 1 + len(parts)
    return call(
        functools.partial(far_final_kernel, layer), 1,
        [SCALARS] + [whole(p.shape) for p in parts] + [ANYWHERE] * len(held), [ANYWHERE, ANYWHERE],
        [struct((LAYERS, E, D // 2), F32), struct((LAYERS, DI // 2, D), F32)],
        [pltpu.VMEM((2, DI, D // 2), F32), pltpu.VMEM((2, DI // 4, D), F32), pltpu.SemaphoreType.DMA((4,))],
        "far_final", deps, aliases={n + k: k for k in range(len(held))},
    )(offs, *parts, *held)


def near_final(offs, parts, layer, held, deps=()):
    n = 1 + len(parts)
    return call(
        functools.partial(near_final_kernel, layer), 1,
        [SCALARS] + [whole(p.shape) for p in parts] + [ANYWHERE], ANYWHERE, struct((LAYERS, E, D // 2), F32),
        [pltpu.VMEM((2, HALF, D // 2), F32), pltpu.SemaphoreType.DMA((3,))],
        "near_final", deps, aliases={n: 0},
    )(offs, *parts, held)


class Sum:
    def __init__(self, offs, name, kernel, args, mid, deps=()):
        rows, width, size = (DI if name == "far_grads" else HALF), D // 2, 256
        block = by_rows((size, width))
        shapes = [(rows, width), (rows, width), (mid, width), ((rows - mid) // 2, 2 * width)]
        self.offs = offs
        self.own, self.away, near, far = call(
            kernel, rows // size, [SCALARS] + [whole(a.shape) for a in args],
            [block, block] + [whole(shape) for shape in shapes[2:]], [struct(shape, BF16) for shape in shapes],
            [], name, deps,
        )(offs, *args)
        self.near, self.far = swap(near, "fsdp"), swap(far, "rep")

    def cross(self, deps=()):
        mid, width = self.near.shape
        first, second = mid // 2, self.far.shape[0]
        shapes = [(first + second, width), (first, width), (second, width)]
        args = (self.own, self.away, self.near, self.far)
        self.keep, to_rep, to_fsdp = call(
            cross_kernel, 1, [SCALARS] + [whole(a.shape) for a in args], [whole(shape) for shape in shapes],
            [struct(shapes[0], F32)] + [struct(shape, BF16) for shape in shapes[1:]], [], "cross", deps,
        )(self.offs, *args)
        self.a, self.b = swap(to_rep, "rep"), swap(to_fsdp, "fsdp")
        return (to_rep,)

    def meet(self, deps=()):
        args = (self.keep, self.a, self.b)
        total = call(
            meet_kernel, 1, [whole(a.shape) for a in args], whole(self.keep.shape), struct(self.keep.shape, BF16),
            [], "meet", deps,
        )(*args)
        self.parts = lax.all_to_all(total, "zz", 0, 0, tiled=True)
        return (total,)

    def reduce(self, deps=()):
        rows, width = self.parts.shape
        count = lax.axis_size("zz")
        copies = reduce_parts(self.parts.reshape(count, rows // count, width), deps)
        self.mine = lax.all_to_all(copies, "zz", 0, 0, tiled=True)
        return (copies,)

    def spread(self, other=None):
        parts = [self.mine, swap(self.mine, "rep") if other is None else other]
        return parts + [swap(p, "core") for p in parts]


def reduce_parts(parts, deps):
    count, rows, width = parts.shape
    return call(
        reduce_kernel, 1, [whole(parts.shape)], whole((count * rows, width)),
        struct((count * rows, width), BF16), [], "reduce_parts", deps,
    )(parts)


def ssd_front(us, rim, segx, taps, heads, oht, copies, deps=()):
    T = us.shape[0]
    nc = T // Q
    return call(
        front_kernel, nc,
        [by_rows((Q, US)), whole((8, CH)), whole(segx.shape), whole(taps.shape),
         whole(heads.shape), whole(oht.shape), whole(copies.shape)],
        [by_rows((Q, ACT)), by_rows((Q, CH)), by_rows((Q, LANES)), by_rows((1, H, Q)),
         by_rows((1, 8, DI)), by_rows((1, N, DI)), whole((N + 8, DI))],
        [struct((T, ACT), BF16), struct((T, CH), BF16), struct((T, LANES), F32), struct((nc, H, Q), F32),
         struct((nc, 8, DI), F32), struct((nc, N, DI), F32), struct((N + 8, DI), F32)],
        [pltpu.VMEM((Q + 8, CH), F32), pltpu.VMEM((N, DI), F32), pltpu.VMEM((8, LANES), F32),
         pltpu.VMEM((Q, DI), BF16)],
        "ssd_front", deps,
    )(us, rim, segx, taps, heads, oht, copies)


def previous(shape):
    return pl.BlockSpec(shape, lambda i: (jnp.maximum(i - 1, 0), 0, 0))


def ssd_within(act, aux, lt, segx, segr, sout, skip, deps=()):
    T = act.shape[0]
    nc = T // Q
    return call(
        within_kernel, nc,
        [by_rows((Q, ACT)), by_rows((Q, LANES)), by_rows((1, H, Q)), whole(segx.shape),
         by_rows((1, 8, LANES)), previous((1, N, DI)), whole(skip.shape)],
        by_rows((Q, DI)), struct((T, DI), F32), [],
        "ssd_within", deps,
    )(act, aux, lt, segx, segr, sout, skip)


def ssd_gate(offs, yloc, aux, drow, s_in, act, z, gain, resid, own, pieces, layer):
    T = yloc.shape[0]
    nc = T // Q
    reads = pl.BlockSpec((Q, N), lambda i: (i, READS.start // N))
    rest = pl.BlockSpec((Q, N), lambda i: (i, READS_REST.start // N))
    return call(
        gate_kernel, nc,
        [SCALARS, by_rows((Q, DI)), by_rows((Q, LANES)), by_rows((1, 8, DI)), whole((N, DI)), reads,
         rest, by_rows((Q, DI)), whole(gain.shape), whole((T, D)),
         pl.BlockSpec((1, DI // 2, D), lambda i: (layer, 0, 0))] + [whole(p.shape) for p in pieces],
        [by_rows((Q, DI)), whole((T, DI // 2)), whole((T, DI // 2)), whole((T, D))],
        [struct((T, DI), F32), struct((T, DI // 2), BF16), struct((T, DI // 2), BF16), struct((T, D), F32)],
        [pltpu.VMEM((Q, DI), F32), pltpu.VMEM((T, DI), BF16)],
        "ssd_gate",
    )(offs, yloc, aux, drow, s_in, act, act, z, gain, resid, own, *pieces)


def gate_back(offs, grad, y, z, gain, act, aux, drow, own, pieces, layer, deps=()):
    T = y.shape[0]
    nc = T // Q
    reads = pl.BlockSpec((Q, N), lambda i: (nc - 1 - i, READS.start // N))
    return call(
        gate_back_kernel, nc,
        [SCALARS, whole((T, D)), by_rows((Q, DI), nc), by_rows((Q, DI), nc), whole(gain.shape), reads,
         by_rows((Q, LANES), nc), by_rows((1, 8, DI), nc),
         pl.BlockSpec((1, DI // 2, D), lambda i: (layer, 0, 0))] + [whole(p.shape) for p in pieces],
        [by_rows((Q, DI), nc)] * 2 + [by_rows((Q, DI // 2), nc)] * 2 + [whole((8, DI)), by_rows((1, N, DI), nc),
         whole((N, DI)), by_rows((1, 8, DI), nc), whole((T, D))],
        [struct((T, DI), BF16)] * 2 + [struct((T, DI // 2), BF16)] * 2
        + [struct((8, DI), F32), struct((nc, N, DI), BF16),
         struct((N, DI), BF16), struct((nc, 8, DI), F32), struct((T, D), BF16)],
        [pltpu.VMEM((Q, DI), F32), pltpu.VMEM((N, DI), F32), pltpu.VMEM((8, DI), F32),
         pltpu.VMEM((Q, DI), BF16), pltpu.VMEM((T, DI), F32), pltpu.VMEM((Q, DI), BF16)],
        "gate_back", deps,
    )(offs, grad, y, z, gain, act, aux, drow, own, *pieces)


def within_back(act, aux, lt, segx, segr, dy, rest, sout, drow, s_in, zloc, deps=()):
    T = act.shape[0]
    nc = T // Q
    return call(
        within_back_kernel, nc,
        [by_rows((Q, ACT)), by_rows((Q, LANES)), by_rows((1, H, Q)), whole(segx.shape),
         by_rows((1, 8, LANES)), by_rows((Q, DI)), by_rows((Q, DI)), previous((1, N, DI)), by_rows((1, 8, DI)),
         whole((N, DI)), by_rows((1, N, DI))],
        [by_rows((Q, DI)), by_rows((Q, 2 * N))],
        [struct((T, DI), F32), struct((T, 2 * N), F32)],
        [pltpu.VMEM((Q, DI), BF16)] * 5,
        "within_back", deps,
    )(act, aux, lt, segx, segr, dy, rest, sout, drow, s_in, zloc)


def ssd_last(offs, act, aux, slope, us, rim, segx, taps, heads, skip, oh, copies, dy, y, dxs, dbc, sout, drow, s_in,
             zloc, dsuf, zdev, deps=()):
    T = act.shape[0]
    nc = T // Q
    return call(
        last_kernel, nc,
        [SCALARS, by_rows((Q, ACT), nc), by_rows((Q, LANES), nc), by_rows((Q, CH), nc), by_rows((Q, US), nc),
         whole((8, CH)), whole(segx.shape), whole(taps.shape),
         whole(heads.shape), whole(skip.shape), whole(oh.shape), whole(copies.shape), by_rows((Q, DI), nc),
         by_rows((Q, DI), nc), by_rows((Q, DI), nc), by_rows((Q, 2 * N), nc), by_rows((1, N, DI), nc),
         by_rows((1, 8, DI), nc), whole((N, DI)), by_rows((1, N, DI), nc), by_rows((1, 8, DI), nc),
         whole((N, DI))],
        [by_rows((Q, HALF), nc)] * 2 + [whole((8, CH)), whole((8, CH)), whole((40, CH)),
         whole((24, LANES))],
        [struct((T, HALF), BF16)] * 2 + [struct((8, CH), F32), struct((8, CH), BF16),
         struct((40, CH), F32), struct((24, LANES), F32)],
        [pltpu.VMEM((Q, CH), BF16), pltpu.VMEM((Q + 8, CH), F32)] + [pltpu.VMEM((Q, DI), BF16)] * 4
        + [pltpu.VMEM((16, DI), F32), pltpu.VMEM((8, DI), F32)],
        "ssd_last", deps,
    )(offs, act, aux, slope, us, rim, segx, taps, heads, skip, oh, copies, dy, y, dxs, dbc, sout, drow, s_in,
      zloc, dsuf, zdev)


def swap(value, axis):
    return lax.ppermute(value, axis, [(0, 1), (1, 0)])


def flip(value, axis, bit):
    size = lax.axis_size(axis)
    return lax.ppermute(value, axis, [(i, i ^ bit) for i in range(size)])


def ordered(index, mine, other, axis):
    return jnp.where(
        index == 0, jnp.concatenate([mine, other], axis), jnp.concatenate([other, mine], axis)
    )


CTX = ("zz", "core")


def routes():
    n = lax.axis_size("zz") * lax.axis_size("core")
    half = n // 2
    first = [(i, i // 2 + (half if i % 2 else 0)) for i in range(n)]
    second = [(i, i // 2 + (0 if i % 2 else half)) for i in range(n)]
    return half, first, second


def gather_tokens(x):
    half, first, second = routes()
    me = lax.axis_index(CTX)
    even = me % 2 == 0
    a = lax.ppermute(jnp.where(even, x[0], x[1]), CTX, first)
    b = lax.ppermute(jnp.where(even, x[1], x[0]), CTX, second)
    early = me < half
    return jnp.concatenate([jnp.where(early, a, b), jnp.where(early, b, a)], axis=0)


def scatter_tokens(x):
    half, first, second = routes()
    me = lax.axis_index(CTX)
    early = me < half
    rows = x.shape[0] // 2
    x0, x1 = x[:rows], x[rows:]
    a = lax.ppermute(jnp.where(early, x0, x1), CTX, [(d, s) for s, d in first])
    b = lax.ppermute(jnp.where(early, x1, x0), CTX, [(d, s) for s, d in second])
    even = me % 2 == 0
    return jnp.stack([jnp.where(even, a, b), jnp.where(even, b, a)])


def next_piece(value, backward=False):
    n = lax.axis_size("zz") * lax.axis_size("core")
    half = n // 2
    pairs = [(i, i + 1) for i in range(n - 1) if i + 1 != half]
    if backward:
        pairs = [(d, s) for s, d in pairs]
    return lax.ppermute(value, CTX, pairs)


def after(value, earlier):
    value, _ = lax.optimization_barrier((value, earlier))
    return value


def fetch(part):
    got = swap(part, "fsdp")
    return got, swap(got, "core")


def carry_forward(core, msg):
    other = swap(msg, "core")

    s_mine, d_mine = msg[:N], msg[N : N + 1]
    s_other, d_other = other[:N], other[N : N + 1]
    lead = core == 0
    s_first, d_first = jnp.where(lead, s_mine, s_other), jnp.where(lead, d_mine, d_other)
    s_second, d_second = jnp.where(lead, s_other, s_mine), jnp.where(lead, d_other, d_mine)
    total = d_second * s_first + s_second
    through = d_first * d_second
    chips = lax.axis_size("zz") // 2
    total = halves(total, core, 0)[0]
    prefix = jnp.zeros_like(total)
    for hop in range(1, chips):
        sent = total if hop == 1 else through * prefix + total
        pairs = [(hop - 1, hop), (chips + hop - 1, chips + hop)]
        prefix = prefix + lax.ppermute(sent, "zz", pairs)
    prefix = ordered(core, prefix, swap(prefix, "core"), 0)
    incoming = jnp.where(lead, prefix, d_first * prefix + s_first)
    return incoming, (d_first, d_second)


def carry_backward(core, msg, decays):
    other = swap(msg, "core")
    d_first, d_second = decays
    lead = core == 0
    g_first = jnp.where(lead, msg, other).astype(F32)
    g_second = jnp.where(lead, other, msg).astype(F32)
    total = g_first + d_first * g_second
    through = d_first * d_second
    chips = lax.axis_size("zz") // 2
    suffix = jnp.zeros_like(total)
    for hop in range(1, chips):
        sent = total if hop == 1 else through * suffix + total
        pairs = [(chips - hop, chips - hop - 1), (2 * chips - hop, 2 * chips - hop - 1)]
        suffix = suffix + lax.ppermute(sent.astype(BF16), "zz", pairs).astype(F32)
    arriving = jnp.where(lead, g_second + d_second * suffix, suffix)
    return arriving.astype(BF16)


def rms_parts(values):
    return lax.rsqrt(jnp.mean(values * values, axis=-1, keepdims=True) + EPSILON)


def halves(array, index, axis):
    size = array.shape[axis] // 2
    mine = lax.dynamic_slice_in_dim(array, index * size, size, axis)
    other = lax.dynamic_slice_in_dim(array, (1 - index) * size, size, axis)
    return mine, other


def levels():
    out = [("rep", 1)]
    bit = 1
    while bit < lax.axis_size("zz"):
        out.append(("zz", bit))
        bit *= 2
    return out


def following(value, *others):
    for other in others:
        mark = other[0, 0]
        value = jnp.where(mark != mark, jnp.zeros_like(value), value)
    return value


def local(
    tokens,
    segments,
    expand_weight,
    reduce_weight,
    filter_taps,
    filter_offset,
    step_bias,
    decay_rate,
    skip_gain,
    norm_gain,
    gate_gain,
    cotangent,
):
    rows = tokens.shape[1]
    T = 2 * rows
    rep = lax.axis_index("rep")
    fsdp = lax.axis_index("fsdp")
    core = lax.axis_index("core")
    me = lax.axis_index(CTX)
    n = lax.axis_size("zz") * lax.axis_size("core")
    half = n // 2

    def pad(x, width):
        return jnp.pad(x, ((0, 0), (0, 0), (0, width - x.shape[-1])))

    expand_t = jnp.swapaxes(expand_weight, 1, 2)
    quarter = D // 4

    def offsets(size):
        start, away = fsdp * size, (1 - fsdp) * size
        zero = jnp.zeros_like(core)
        return jnp.stack(
            [start, away + core * (size // 2), away + (1 - core) * (size // 2), zero, zero, zero, rep, core]
        ).astype(jnp.int32)

    offs, wide_offs = offsets(D // 2), offsets(DI // 2)

    def take_lanes(layer, start, rows, deps):
        size = 512
        return call(
            functools.partial(take_kernel, True), -(-rows // size),
            [SCALARS, pl.BlockSpec((1, size, D // 2), lambda i: (layer, start // size + i, 0))],
            by_rows((size, quarter)), struct((rows, quarter), BF16), [], "take", deps,
        )(offs, expand_t)

    first_taken = take_lanes(0, DI, US, ())
    heads_packed = jnp.concatenate([step_bias, decay_rate, skip_gain], axis=-1)
    own = jnp.concatenate(
        [filter_taps, filter_offset[:, None], pad(norm_gain[:, None], CH // 2),
         pad(gate_gain[:, None], CH // 2), pad(heads_packed[:, None], CH // 2)], axis=1
    )
    other = swap(following(own, first_taken), "fsdp")
    lead = fsdp == 0
    low_half = jnp.where(lead, own, other).astype(F32)
    high_half = jnp.where(lead, other, own).astype(F32)

    def joined(row, start, size):
        return jnp.concatenate(
            [low_half[:, row, start : start + size], high_half[:, row, start : start + size]], axis=-1
        )

    taps_all = jnp.concatenate([low_half[:, :5], high_half[:, :5]], axis=-1)
    taps_all = jnp.pad(taps_all, ((0, 0), (0, 3), (0, 0)))
    norm_all, gate_all = joined(5, 0, D // 2), joined(6, 0, DI // 2)
    bias_all, rate_all, skip_all = joined(7, 0, H // 2), joined(7, H // 2, H // 2), joined(7, H, H // 2)
    heads_all = jnp.pad(
        jnp.stack([jnp.tile(bias_all, (1, 4)), jnp.tile(rate_all, (1, 4))], axis=1), ((0, 0), (0, 6), (0, 0))
    )
    skip_rows = jnp.repeat(skip_all, P_SIZE, axis=-1)

    hot = (
        lax.broadcasted_iota(jnp.int32, (DI, LANES), 0) // P_SIZE
        == lax.broadcasted_iota(jnp.int32, (DI, LANES), 1)
    ).astype(BF16)
    hot_t = (
        lax.broadcasted_iota(jnp.int32, (LANES, DI), 1) // P_SIZE
        == lax.broadcasted_iota(jnp.int32, (LANES, DI), 0)
    ).astype(BF16)

    copies = (
        lax.broadcasted_iota(jnp.int32, (H, LANES), 0) == lax.broadcasted_iota(jnp.int32, (H, LANES), 1) % H
    ).astype(BF16)

    seq = (me >= half).astype(jnp.int32)
    padded = jnp.pad(segments, ((0, 0), (8, 8)), constant_values=-1)
    seg_line = lax.dynamic_slice(padded, (seq, (me % half) * T), (1, T + 16))[0].astype(F32)
    segx = jnp.broadcast_to(seg_line[:, None], (T + 16, LANES))
    segr = jnp.broadcast_to(seg_line[8 : 8 + T].reshape(T // Q, 1, Q), (T // Q, 8, Q))

    def take_rows(layer, deps):
        return call(
            functools.partial(take_kernel, False), 1,
            [SCALARS, pl.BlockSpec((1, DI // 2, D), lambda i: (layer, 0, 0))],
            whole((DI // 4, D)), struct((DI // 4, D), BF16), [], "take", deps,
        )(offs, reduce_weight)


    def fetch_layer(layer, near, after_far=(), after_rows=()):
        far = take_lanes(layer, 0, DI, after_far + (near,))
        rows_of = take_rows(layer, after_rows + (far,))
        return fetch(far), fetch(rows_of)

    weights = [(fetch(first_taken),) + fetch_layer(0, first_taken)]

    resid = gather_tokens(following(tokens, first_taken)).astype(F32)
    saved, out_both = [], ()
    for layer in range(LAYERS):
        near, far, rows_of = weights[layer]
        us, normed = expand_first(offs, resid, norm_all[layer][None], expand_t, near, layer)
        rim = us[T - 8 :, :CH]
        rim = next_piece(following(rim, far_cotangent) if layer else rim)
        taps, heads = taps_all[layer], heads_all[layer]
        skip = skip_rows[layer][None]
        next_taken = (take_lanes(layer + 1, DI, US, (us,)),) if layer + 1 < LAYERS else ()
        act, slope, aux, lt, drow, sout, msg = ssd_front(us, rim, segx, taps, heads, hot_t, copies, out_both[1:] + next_taken)
        z = expand_rest(offs, normed, expand_t, far, layer, (act,))
        s_in, decays = carry_forward(core, following(msg, far[0]) if layer else msg)
        normed_both = normed, swap(normed, "core")
        within_deps = normed_both[1:]
        if layer == 0:
            far_cotangent = gather_tokens(following(cotangent, s_in))
            grad = far_cotangent.astype(F32)
        else:
            within_deps += (rows_of[0],)
        yloc = ssd_within(act, aux, lt, segx, segr, sout, skip, within_deps)
        if layer + 1 < LAYERS:
            weights.append((fetch(next_taken[0]),) + fetch_layer(layer + 1, next_taken[0], (act,), (yloc,)))
        gain = gate_all[layer][None]
        y, out_mine, out_other, resid_next = ssd_gate(
            wide_offs, yloc, aux, drow, s_in, act, z, gain, resid, reduce_weight, rows_of, layer
        )
        out_both = out_mine, swap(out_other, "core")
        saved.append((resid, normed_both, z, us, rim, act, slope, aux, lt, drow, sout, s_in, decays, y, out_both))
        resid = resid_next
    layer_out = scatter_tokens(resid.astype(BF16))

    small = [None] * LAYERS
    far_sums, near_sums, pending = {}, {}, ()

    for layer in reversed(range(LAYERS)):
        near, far, rows_of = weights[layer]
        (resid_in, normed_both, z, us, rim, act, slope, aux, lt, drow, sout, s_in, decays, y, out_both) = saved[layer]
        taps, heads = taps_all[layer], heads_all[layer]
        skip = skip_rows[layer][None]
        gain = gate_all[layer][None]
        first = layer == 0
        dy, dy_rest, dzm, dzo, ggrad, zloc, gmsg, dsuf, grad_low = gate_back(
            wide_offs, grad, y, z, gain, act, aux, drow, reduce_weight, rows_of, layer, pending
        )
        arrived = near_sums[1].cross((gmsg,)) if first else ()
        if first:
            gmsg = following(gmsg, *arrived, far_sums[1].mine)
        zdev = carry_backward(core, gmsg, decays)
        far_args = (dzm, swap(dzo, "core"), *normed_both, *out_both, grad_low, swap(grad_low, "core"))
        far_sums[layer] = Sum(offs, "far_grads", far_grads_kernel, far_args, FAR_MID, arrived)
        before = (far_sums[layer].own,)
        if first:
            before += near_sums[1].meet((zdev,) + before)
        dxs, dbc = within_back(act, aux, lt, segx, segr, dy, dy_rest, sout, drow, s_in, zloc, before)
        before = far_sums[layer].cross((dxs,))
        if first:
            before += (far_sums[1].mine,) + near_sums[1].reduce((dxs,))
        dum, duo, tail, rimout, tgrad, hgrad = ssd_last(
            offs, act, aux, slope, us, rim, segx, taps, heads, skip, hot, copies, dy, y, dxs, dbc, sout, drow, s_in,
            zloc, dsuf, zdev, before
        )
        token = (near_sums[1].mine,) if first else far_sums[1].meet((dum,)) + (layer_out[0],)
        rimout = following(rimout, *token)
        tail = (tail + next_piece(rimout, True).astype(F32)).astype(BF16)
        tail_mine, tail_other = halves(tail, core, 1)
        dum = lax.dynamic_update_slice(dum, tail_mine, (T - 8, 0))
        duo = lax.dynamic_update_slice(duo, tail_other, (T - 8, 0))
        near_args = (dum, swap(duo, "core"), *normed_both)
        if first:
            token = far_sums[0].meet(near_args[1:2])
            near_sums[0] = Sum(offs, "near_grads", near_grads_kernel, near_args, NEAR_MID, token)
            token = (near_sums[0].own,)
        grad, ngrad = input_back(
            offs, dzm, dzo, dum, duo, norm_all[layer][None], resid_in, grad, expand_t, near, far, layer, token
        )
        if not first:
            token = far_sums[1].reduce((grad,))
            near_sums[1] = Sum(offs, "near_grads", near_grads_kernel, near_args, NEAR_MID, token)
            pending = (near_sums[1].own,)
        tgrad = jnp.sum(tgrad.reshape(5, 8, CH), axis=1).reshape(-1)
        hgrad = jnp.sum(hgrad.reshape(3, 8, LANES), axis=1)[:, :H].reshape(-1)
        small[layer] = jnp.concatenate([tgrad, jnp.sum(ggrad, axis=0), jnp.sum(ngrad, axis=0), hgrad])

    size = small[0].shape[0]
    padded_size = -(-size // 1024) * 1024
    packed = jnp.pad(jnp.stack(small), ((0, 0), (0, padded_size - size))).reshape(-1, LANES)
    hops = [("core", 1)] + levels() + [("fsdp", 1)]

    def hop(packed):
        axis, bit = hops.pop(0)
        return packed + flip(packed, axis, bit)

    far_other = swap(far_sums[1].mine, "rep")
    token = far_sums[0].reduce((grad, far_other))
    packed = hop(packed)
    token = near_sums[0].cross(token + (packed,))
    near_other = swap(near_sums[1].mine, "rep")
    packed = hop(packed)
    token = near_sums[0].meet(token + (far_sums[0].mine, near_other, packed))
    first_other = swap(far_sums[0].mine, "rep")
    expand_sum, reduce_sum = far_final(offs, far_sums[1].spread(far_other), 1, (), token)
    expand_sum = near_final(offs, near_sums[1].spread(near_other), 1, expand_sum)
    packed = hop(packed)
    token = near_sums[0].reduce(token + (first_other, packed, expand_sum))
    packed = hop(packed)
    expand_sum, reduce_sum = far_final(
        offs, far_sums[0].spread(first_other), 0, (expand_sum, reduce_sum), token + (packed,)
    )
    token_grads = scatter_tokens(following(grad.astype(BF16), near_sums[0].mine))
    while hops:
        packed = hop(packed)
    expand_sum = near_final(offs, near_sums[0].spread(), 0, expand_sum)
    packed = packed.reshape(LAYERS, padded_size)

    def own_half(x):
        return halves(x, fsdp, x.ndim - 1)[0]

    tap_grads = own_half(packed[:, : 4 * CH].reshape(LAYERS, 4, CH))
    offset_grads = own_half(packed[:, 4 * CH : 5 * CH])
    at = 5 * CH
    gating_grads = own_half(packed[:, at : at + DI])
    at += DI
    norm_grads = own_half(packed[:, at : at + D])
    at += D
    step_grads = own_half(packed[:, at : at + H])
    decay_grads = own_half(packed[:, at + H : at + 2 * H])
    skip_grads = own_half(packed[:, at + 2 * H : at + 3 * H])

    return (
        layer_out,
        token_grads,
        jnp.swapaxes(expand_sum, 1, 2),
        reduce_sum,
        tap_grads,
        offset_grads,
        step_grads,
        decay_grads,
        skip_grads,
        norm_grads,
        gating_grads,
    )


def solution(mesh):
    rep, fsdp, ctx = (mesh.shape[name] for name in ("rep", "fsdp", "ctx"))
    inner = Mesh(mesh.devices.reshape(rep, fsdp, ctx // 2, 2), ("rep", "fsdp", "zz", "core"))
    tokens = P(("rep", "fsdp"), ("zz", "core"), None)
    first, last = P(None, "fsdp"), P(None, None, "fsdp")
    return jax.shard_map(
        local,
        mesh=inner,
        in_specs=(
            tokens, P(("rep", "fsdp"), None), P(None, "fsdp", None), P(None, "fsdp", None), last,
            first, first, first, first, first, first, tokens,
        ),
        out_specs=(
            tokens, tokens, P(None, "fsdp", None), P(None, "fsdp", None), last,
            first, first, first, first, first, first,
        ),
        check_vma=False,
    )
```
